128 devices in a mesh: ctx: 16 (over x, z), ch: 8 (over y, core).
Axes of the slice: x: 4, y: 4, z: 4, core: 2. Of those that a mesh axis runs over, the one named last changes fastest.
Arguments:
- conv_input: bfloat16 [8192, 8192], P('ctx', 'ch'), may hold values from -6 to 6
- out_gate: bfloat16 [8192, 8192], P('ctx', 'ch'), may hold values from -6 to 6
- grad_out: bfloat16 [8192, 8192], P('ctx', 'ch'), may hold values from -6 to 6
- pole_rate: float32 [16, 8192], P(None, 'ch'), may hold values from 0 to 1, as said below
- residue: float32 [16, 8192], P(None, 'ch'), may hold values from -1 to 1
- skip_gain: float32 [8192], P('ch'), may hold values from -3 to 3
Outputs:
- input_grad: bfloat16 [8192, 8192], P('ctx', 'ch')
- gate_grad: bfloat16 [8192, 8192], P('ctx', 'ch')
- residue_grad: float32 [16, 8192], P(None, 'ch')
- lograte_grad: float32 [16, 8192], P(None, 'ch')
- skip_grad: float32 [8192], P('ch')
The draws below stay inside these ranges and needn't reach their ends.
Inputs may be any that keep to these rules, and one draw needn't show every extreme that they name: Positive decay rates; for every pole, exp(-pole_rate) lies in (0, 1).
All inputs are finite; a program needn't handle non-finite values.
Results may differ from the reference program's by a relative error of at most 0.0015.
Values sent between devices are 32-bit elements; how exact they have to be, the bound alone decides.
No kernel may reach another device: no remote copies, remote signals or barrier semaphores. Data moves between devices by JAX's collectives and lax.ppermute only.
A program may use at most 320 MiB of HBM per device.

```python
import math
import jax
import jax.numpy as jnp
from jax import lax

CHANNELS = 8192
MODES = 16
TOKENS = 8192


def mode_rates(key, slow_share):
    chooser, slow_key, fast_key = jax.random.split(key, 3)
    table_shape = (MODES, CHANNELS)
    is_slow = jax.random.uniform(chooser, table_shape) < slow_share
    slow_rate = jnp.exp(jax.random.uniform(slow_key, table_shape, minval=jnp.log(0.2 / TOKENS), maxval=jnp.log(2.0 / TOKENS)))
    fast_rate = jnp.exp(jax.random.uniform(fast_key, table_shape, minval=jnp.log(2.0 / TOKENS), maxval=jnp.log(1.0 / 30.0)))
    return jnp.where(is_slow, slow_rate, fast_rate).astype(jnp.float32)


def draw_pole_rate(key, part):
    slow_share = 0.5
    return mode_rates(key, slow_share)


def draw_residue(key, part):
    slow_share = 0.5
    rates = mode_rates(key, slow_share)
    key = jax.random.fold_in(key, 7)
    values = jnp.clip(jax.random.normal(key, (MODES, CHANNELS), jnp.float32), -4.0, 4.0)
    return (values * 0.5 * jnp.sqrt(1.0 - jnp.exp(-2.0 * rates))).astype(jnp.float32)


def steps_of(rng, dims, cuts, low, high):
    def one(position, blocks):
        heights = jax.random.uniform(jax.random.fold_in(jax.random.fold_in(rng, 6), position), (blocks,), jnp.float32, low / len(cuts), high / len(cuts))
        return jnp.repeat(jnp.exp(heights), dims[position] // blocks).reshape((-1,) + (1,) * (len(dims) - position - 1))

    loudness = one(*cuts[0])
    for cut in cuts[1:]:
        loudness = loudness * one(*cut)
    return loudness


def scatter_about(own_key, dims, scale, reach, shards=(), kind=jnp.bfloat16):
    entries = scale * jax.random.normal(own_key, dims, jnp.float32)
    if shards:
        entries = entries * steps_of(own_key, dims, shards, -0.22, 0.18)
    return jnp.clip(entries, -reach, reach).astype(kind)


def setup_inputs(seed: int = 0) -> dict:
    streams_of = jax.random.split(jax.random.key(seed), 7)
    conv_input = scatter_about(streams_of[0], (TOKENS, CHANNELS), 1.0, 6.0, ((0, 16), (1, 8)))
    out_gate = scatter_about(streams_of[1], (TOKENS, CHANNELS), 1.0, 6.0, ((0, 16), (1, 8)))
    grad_out = scatter_about(streams_of[2], (TOKENS, CHANNELS), 1.0, 6.0, ((0, 16), (1, 8)))
    pole_rate = draw_pole_rate(jax.random.fold_in(streams_of[6], 71), 0)
    residue = draw_residue(jax.random.fold_in(streams_of[6], 71), 0)
    skip_gain = scatter_about(streams_of[5], (CHANNELS,), 0.5, 3.0, ((0, 8),), jnp.float32)
    return {"conv_input": conv_input, "out_gate": out_gate, "grad_out": grad_out, "pole_rate": pole_rate, "residue": residue, "skip_gain": skip_gain}


def clip_factor(total_sq, ceiling):
    return jnp.minimum(1.0, ceiling / jnp.sqrt(total_sq + 1e-06))

def reference(conv_input, out_gate, grad_out, pole_rate, residue, skip_gain):
    decays = jnp.exp(-pole_rate)
    zero_state = jnp.zeros_like(decays)
    zero_skip = jnp.zeros_like(skip_gain)

    def forward_step(carried, rows_in):
        state_now, sense_now, res_acc, sense_acc, skip_acc = carried
        input_row = rows_in[0].astype(jnp.float32)
        grad_row = rows_in[2].astype(jnp.float32)
        signal_row = grad_row * rows_in[1].astype(jnp.float32)
        sense_now = decays * sense_now + state_now
        state_now = decays * state_now + input_row[None, :]
        mixed_row = lax.optimization_barrier(jnp.sum(residue * state_now, axis=0)) + skip_gain * input_row
        res_acc = res_acc + signal_row[None, :] * state_now
        sense_acc = sense_acc + signal_row[None, :] * sense_now
        skip_acc = skip_acc + signal_row * input_row
        return ((state_now, sense_now, res_acc, sense_acc, skip_acc), (grad_row * mixed_row).astype(jnp.bfloat16))
    start = (zero_state, zero_state, zero_state, zero_state, zero_skip)
    totals, gate_grad = lax.scan(forward_step, start, (conv_input, out_gate, grad_out))
    res_raw = totals[2]
    log_raw = -decays * pole_rate * residue * totals[3]
    skip_raw = totals[4]

    def backward_step(adjoint, rows_in):
        signal_row = rows_in[1].astype(jnp.float32) * rows_in[0].astype(jnp.float32)
        adjoint = decays * adjoint + signal_row[None, :]
        back_row = lax.optimization_barrier(jnp.sum(residue * adjoint, axis=0)) + skip_gain * signal_row
        return (adjoint, back_row.astype(jnp.bfloat16))
    final_adjoint, input_grad = lax.scan(backward_step, zero_state, (out_gate, grad_out), reverse=True)
    limit_modes = math.sqrt(MODES * CHANNELS)
    limit_skip = math.sqrt(CHANNELS)
    residue_grad = res_raw * clip_factor(jnp.sum(res_raw * res_raw), limit_modes)
    lograte_grad = log_raw * clip_factor(jnp.sum(log_raw * log_raw), limit_modes)
    skip_grad = skip_raw * clip_factor(jnp.sum(skip_raw * skip_raw), limit_skip)
    return (input_grad, gate_grad, residue_grad, lograte_grad, skip_grad)
```

```python
import functools
import math

import jax
import jax.numpy as jnp
from jax import lax
from jax.experimental import pallas as pl
from jax.experimental.pallas import tpu as pltpu
from jax.sharding import PartitionSpec as P

CHANNELS = 8192
MODES = 16
LANES = 128
SEGS = 8
SUB = 8
F32 = jnp.float32
VMEM_LIMIT = 48 * 1024 * 1024


def rows_of(ref, start, count, stride):
    return ref[pl.ds(start, count, stride=stride), :]


def spread(ref_out, values):
    for m in range(MODES):
        ref_out[m] = jnp.broadcast_to(values[m : m + 1, :], (SEGS, LANES))


def by_segment(natural, ordered, seg_len):
    for q in range(seg_len):
        ordered[q] = rows_of(natural, q, SEGS, seg_len)


def span_kernel(
    x_ref, o_ref, g_ref, rate_ref, res_ref,
    hl_ref, al_ref, hs_ref, as_ref, pay_ref,
    natural, xq, sq, lam_t, mu_t, rl_t, ends,
):
    tokens = x_ref.shape[0]
    seg_len = tokens // SEGS
    chunks = seg_len // SUB
    group = pl.program_id(0)
    rate = rate_ref[...]
    lam = jnp.exp(-rate)
    spread(lam_t, lam)
    spread(mu_t, jnp.exp(rate * (-float(SUB))))
    spread(rl_t, res_ref[...] * lam)

    source = x_ref[...].astype(F32)
    natural[...] = source
    by_segment(natural, xq, seg_len)
    signal = g_ref[...].astype(F32) * o_ref[...].astype(F32)
    skip_row = jnp.sum(source * signal, axis=0, keepdims=True)
    natural[...] = signal
    by_segment(natural, sq, seg_len)

    def lag_step(k, acc):
        xs = [xq[k * SUB + j] for j in range(SUB)]
        ss = [sq[k * SUB + j] for j in range(SUB)]
        out = []
        for d in range(SUB):
            total = acc[d]
            for i in range(d, SUB):
                total = total + ss[i] * xs[i - d]
            out.append(total)
        return tuple(out)

    zero = jnp.zeros((SEGS, LANES), F32)
    lagged = lax.fori_loop(0, chunks, lag_step, (zero,) * SUB)
    lag_rows = [jnp.sum(v, axis=0, keepdims=True) for v in lagged]
    res_near = jnp.broadcast_to(lag_rows[0], lam.shape)
    log_near = jnp.zeros_like(lam)
    power = lam
    for d in range(1, SUB):
        term = power * lag_rows[d]
        res_near = res_near + term
        log_near = log_near + float(d) * term
        power = power * lam

    def mode_step(m, carry):
        p1 = lam_t[m]
        mu = mu_t[m]
        rl = rl_t[m]
        p2 = p1 * p1
        p3 = p2 * p1
        p4 = p2 * p2
        pw = [None, p1, p2, p3, p4, p4 * p1, p3 * p3, p4 * p3]
        a_run = zero
        b_run = zero
        a_parts = [None] * chunks
        b_parts = [None] * chunks
        for k in reversed(range(chunks)):
            al_ref[0, k, m] = rl * a_run
            a = sq[k * SUB + SUB - 1] * pw[SUB - 1]
            b = a
            for i in reversed(range(1, SUB - 1)):
                a = a + sq[k * SUB + i] * pw[i]
                b = b + a
            a = a + sq[k * SUB]
            a_parts[k] = a
            b_parts[k] = b
            b_run = b + mu * (b_run + float(SUB) * a_run)
            a_run = a + mu * a_run
        h_run = zero
        p_run = zero
        res_x = zero
        log_x = zero
        for k in range(chunks):
            hl_ref[0, k, m] = rl * h_run
            h = xq[k * SUB] * pw[SUB - 1]
            p = h
            for j in range(1, SUB - 1):
                h = h + xq[k * SUB + j] * pw[SUB - 1 - j]
                p = p + h
            h = h + xq[k * SUB + SUB - 1]
            if k == 0:
                h_run = h
                p_run = p
            else:
                res_x = res_x + h_run * a_parts[k]
                log_x = log_x + (p_run * a_parts[k] + h_run * b_parts[k])
                p_run = p + mu * (p_run + float(SUB) * h_run)
                h_run = h + mu * h_run
        for n, value in enumerate((h_run, p_run, a_run, b_run, res_x, log_x)):
            ends[n, pl.ds(pl.multiple_of(m * SEGS, SEGS), SEGS), :] = value
        return carry

    lax.fori_loop(0, MODES, mode_step, 0)

    def end(n, s):
        return ends[n, pl.ds(s, MODES, stride=SEGS), :]

    big = jnp.exp(rate * (-float(seg_len)))
    span = float(seg_len)
    nothing = jnp.zeros_like(lam)
    h, p, res_x, log_x = nothing, nothing, nothing, nothing
    for s in range(SEGS):
        hs_ref[0, s] = h
        a_s, b_s = end(2, s), end(3, s)
        res_x = res_x + end(4, s) + h * a_s
        log_x = log_x + end(5, s) + (p * a_s + h * b_s)
        p = end(1, s) + big * (p + span * h)
        h = end(0, s) + big * h
    a, b = nothing, nothing
    for s in reversed(range(SEGS)):
        as_ref[0, s] = a
        b = end(3, s) + big * (b + span * a)
        a = end(2, s) + big * a
    res_sum = lam * res_x + res_near
    log_sum = lam * (log_x + res_x) + log_near
    rows = (h, p, a, b, res_sum, log_sum, jnp.broadcast_to(skip_row, lam.shape), rate)
    for n, value in enumerate(rows):
        pay_ref[pl.ds(n * 8 + group, MODES, stride=64), :] = value


def chain_kernel(tokens, got_ref, back_ref, skip_ref):
    spans = got_ref.shape[0]

    def part(d, n):
        return got_ref[d, pl.ds(8 * n, 8), :]

    rate = part(0, 7)
    lam = jnp.exp(-rate)
    big = jnp.exp(rate * (-float(tokens)))
    span = float(tokens)
    zero = jnp.zeros((8, LANES), F32)
    h, p, res_x, log_x, res_sum, log_sum, skip = (zero,) * 7
    for d in range(spans):
        back_ref[d, pl.ds(0, 8), :] = h
        a_d = part(d, 2)
        res_x = res_x + h * a_d
        log_x = log_x + (p * a_d + h * part(d, 3))
        res_sum = res_sum + part(d, 4)
        log_sum = log_sum + part(d, 5)
        skip = skip + part(d, 6)
        p = part(d, 1) + big * (p + span * h)
        h = part(d, 0) + big * h
    a = zero
    for d in reversed(range(spans)):
        back_ref[d, pl.ds(8, 8), :] = a
        a = part(d, 2) + big * a
    res_total = res_sum + lam * res_x
    log_total = log_sum + lam * (log_x + res_x)
    for d in range(spans):
        back_ref[d, pl.ds(16, 8), :] = res_total
        back_ref[d, pl.ds(24, 8), :] = log_total
    skip_ref[...] = skip


def out_kernel(
    x_ref, o_ref, g_ref, rate_ref, res_ref, gain_ref, hl_ref, al_ref, hs_ref, as_ref, back_ref,
    ig_ref, gg_ref,
    natural, second, xq, sq, lam_t, mu_t, near_t, gh, ga,
):
    tokens = x_ref.shape[0]
    seg_len = tokens // SEGS
    chunks = seg_len // SUB
    group = pl.program_id(0)
    rate = rate_ref[...]
    residue = res_ref[...]
    lam = jnp.exp(-rate)
    spread(lam_t, lam)
    spread(mu_t, jnp.exp(rate * (-float(SUB))))
    rl = residue * lam
    h_in = rows_of(back_ref, group, MODES, 32)
    a_in = rows_of(back_ref, 8 + group, MODES, 32)
    big = jnp.exp(rate * (-float(seg_len)))
    for s in range(SEGS):
        gh[pl.ds(s, MODES, stride=SEGS), :] = rl * (hs_ref[0, s] + h_in)
        h_in = h_in * big
    for s in reversed(range(SEGS)):
        ga[pl.ds(s, MODES, stride=SEGS), :] = rl * (as_ref[0, s] + a_in)
        a_in = a_in * big
    term = residue
    for d in range(SUB):
        row = jnp.sum(term, axis=0, keepdims=True)
        if d == 0:
            row = row + gain_ref[...]
        near_t[d] = jnp.broadcast_to(row, (SEGS, LANES))
        term = term * lam

    natural[...] = x_ref[...].astype(F32)
    by_segment(natural, xq, seg_len)
    second[...] = g_ref[...].astype(F32) * o_ref[...].astype(F32)
    by_segment(second, sq, seg_len)

    def chunk_step(k, carry):
        kb = chunks - 1 - k
        near = [near_t[d] for d in range(SUB)]
        xs = [xq[k * SUB + j] for j in range(SUB)]
        out = []
        for i in range(SUB):
            total = near[0] * xs[i]
            for d in range(1, i + 1):
                total = total + near[d] * xs[i - d]
            out.append(total)
        ss = [sq[kb * SUB + j] for j in range(SUB)]
        back = []
        for j in range(SUB):
            total = near[0] * ss[j]
            for d in range(1, SUB - j):
                total = total + near[d] * ss[j + d]
            back.append(total)
        for m in range(MODES):
            here = pl.ds(m * SEGS, SEGS)
            step, mu = lam_t[m], mu_t[m]
            g = gh[here, :]
            c = hl_ref[0, k, m] + g
            gh[here, :] = g * mu
            for i in range(SUB):
                out[i] = out[i] + c
                if i < SUB - 1:
                    c = c * step
            g = ga[here, :]
            c = al_ref[0, kb, m] + g
            ga[here, :] = g * mu
            for i in reversed(range(SUB)):
                back[i] = back[i] + c
                if i > 0:
                    c = c * step
        for i in range(SUB):
            natural[pl.ds(k * SUB + i, SEGS, stride=seg_len), :] = out[i]
            second[pl.ds(kb * SUB + i, SEGS, stride=seg_len), :] = back[i]
        return carry

    lax.fori_loop(0, chunks, chunk_step, 0)
    gg_ref[...] = (g_ref[...].astype(F32) * natural[...]).astype(jnp.bfloat16)
    ig_ref[...] = second[...].astype(jnp.bfloat16)


def totals(back_ref, rate_ref, res_ref, group):
    cols = pl.ds(group * LANES, LANES)
    res_raw = rows_of(back_ref, 16 + group, MODES, 32)
    log_raw = -(rate_ref[:, cols] * res_ref[:, cols]) * rows_of(back_ref, 24 + group, MODES, 32)
    return res_raw, log_raw


def norm_kernel(back_ref, skip_ref, rate_ref, res_ref, sq_ref):
    groups = skip_ref.shape[0]
    res_sq = jnp.zeros((MODES, LANES), F32)
    log_sq = jnp.zeros((MODES, LANES), F32)
    for group in range(groups):
        res_raw, log_raw = totals(back_ref, rate_ref, res_ref, group)
        res_sq = res_sq + res_raw * res_raw
        log_sq = log_sq + log_raw * log_raw
    skip = skip_ref[...]
    rows = [jnp.sum(v, axis=0, keepdims=True) for v in (res_sq, log_sq, skip * skip)]
    sq_ref[...] = jnp.concatenate(rows + [jnp.zeros((5, LANES), F32)], axis=0)


def scale_kernel(all_sq_ref, back_ref, skip_ref, rate_ref, res_ref, rg_ref, lg_ref, sg_ref):
    groups = skip_ref.shape[0]
    sums = jnp.sum(jnp.sum(all_sq_ref[...], axis=0), axis=1, keepdims=True)

    def factor(n, ceiling):
        return jnp.minimum(1.0, ceiling / jnp.sqrt(sums[n : n + 1, :] + 1e-06))

    limit_modes = math.sqrt(MODES * CHANNELS)
    res_factor = factor(0, limit_modes)
    log_factor = factor(1, limit_modes)
    for group in range(groups):
        cols = pl.ds(group * LANES, LANES)
        res_raw, log_raw = totals(back_ref, rate_ref, res_ref, group)
        rg_ref[:, cols] = res_raw * res_factor
        lg_ref[:, cols] = log_raw * log_factor
    sg_ref[...] = skip_ref[...] * factor(2, math.sqrt(CHANNELS))


def params():
    return pltpu.CompilerParams(vmem_limit_bytes=VMEM_LIMIT)


def on_device(conv_input, out_gate, grad_out, pole_rate, residue, skip_gain):
    tokens, chan = conv_input.shape
    groups = chan // LANES
    seg_len = tokens // SEGS
    chunks = seg_len // SUB
    spans = lax.axis_size("ctx")
    wide = pl.BlockSpec((tokens, LANES), lambda g: (0, g))
    modal = pl.BlockSpec((MODES, LANES), lambda g: (0, g))
    chunked = pl.BlockSpec((1, chunks, MODES, SEGS, LANES), lambda g: (g, 0, 0, 0, 0))
    segged = pl.BlockSpec((1, SEGS, MODES, LANES), lambda g: (g, 0, 0, 0))
    chunked_shape = jax.ShapeDtypeStruct((groups, chunks, MODES, SEGS, LANES), F32)
    segged_shape = jax.ShapeDtypeStruct((groups, SEGS, MODES, LANES), F32)
    ordered = pltpu.VMEM((seg_len, SEGS, LANES), F32)
    natural = pltpu.VMEM((tokens, LANES), F32)
    table = pltpu.VMEM((MODES, SEGS, LANES), F32)

    hl, al, hs, as_, pay = pl.pallas_call(
        span_kernel,
        grid=(groups,),
        in_specs=[wide, wide, wide, modal, modal],
        out_specs=[
            chunked, chunked, segged, segged,
            pl.BlockSpec((MODES * 64, LANES), lambda g: (0, 0)),
        ],
        out_shape=[
            chunked_shape, chunked_shape, segged_shape, segged_shape,
            jax.ShapeDtypeStruct((MODES * 64, LANES), F32),
        ],
        scratch_shapes=[
            natural, ordered, ordered, table, table, table,
            pltpu.VMEM((6, MODES * SEGS, LANES), F32),
        ],
        compiler_params=params(),
        name="span",
    )(conv_input, out_gate, grad_out, pole_rate, residue)

    got = lax.all_to_all(pay.reshape(spans, 64, LANES), "ctx", 0, 0)
    back, skip_raw = pl.pallas_call(
        functools.partial(chain_kernel, tokens),
        out_shape=[
            jax.ShapeDtypeStruct((spans, 32, LANES), F32),
            jax.ShapeDtypeStruct((groups, LANES), F32),
        ],
        compiler_params=params(),
        name="chain",
    )(got)
    back = lax.all_to_all(back, "ctx", 0, 0).reshape(MODES * 32, LANES)

    part_sq = pl.pallas_call(
        norm_kernel,
        out_shape=jax.ShapeDtypeStruct((8, LANES), F32),
        compiler_params=params(),
        name="norm",
    )(back, skip_raw, pole_rate, residue)
    all_sq = lax.all_gather(part_sq, "ch")

    input_grad, gate_grad = pl.pallas_call(
        out_kernel,
        grid=(groups,),
        in_specs=[
            wide, wide, wide, modal, modal,
            pl.BlockSpec((1, LANES), lambda g: (0, g)),
            chunked, chunked, segged, segged,
            pl.BlockSpec((MODES * 32, LANES), lambda g: (0, 0)),
        ],
        out_specs=[wide, wide],
        out_shape=[jax.ShapeDtypeStruct((tokens, chan), jnp.bfloat16)] * 2,
        scratch_shapes=[
            natural, natural, ordered, ordered, table, table,
            pltpu.VMEM((SUB, SEGS, LANES), F32),
            pltpu.VMEM((MODES * SEGS, LANES), F32),
            pltpu.VMEM((MODES * SEGS, LANES), F32),
        ],
        compiler_params=params(),
        name="outs",
    )(
        conv_input, out_gate, grad_out, pole_rate, residue, skip_gain.reshape(1, chan),
        hl, al, hs, as_, back,
    )

    res_out, log_out, skip_out = pl.pallas_call(
        scale_kernel,
        out_shape=[
            jax.ShapeDtypeStruct((MODES, chan), F32),
            jax.ShapeDtypeStruct((MODES, chan), F32),
            jax.ShapeDtypeStruct((groups, LANES), F32),
        ],
        compiler_params=params(),
        name="scale",
    )(all_sq, back, skip_raw, pole_rate, residue)
    return input_grad, gate_grad, res_out, log_out, skip_out.reshape(chan)


def solution(mesh):
    in_specs = (
        P("ctx", "ch"), P("ctx", "ch"), P("ctx", "ch"), P(None, "ch"), P(None, "ch"), P("ch"),
    )
    out_specs = (P("ctx", "ch"), P("ctx", "ch"), P(None, "ch"), P(None, "ch"), P("ch"))
    return jax.shard_map(
        on_device, mesh=mesh, in_specs=in_specs, out_specs=out_specs, check_vma=False
    )
```

```python
import functools
import math

import jax
import jax.numpy as jnp
from jax import lax
from jax.experimental import pallas as pl
from jax.experimental.pallas import tpu as pltpu
from jax.sharding import PartitionSpec as P

CHANNELS = 8192
MODES = 16
LANES = 128
SEGS = 8
SUB = 8
F32 = jnp.float32
PITCH = 72
VMEM_LIMIT = 24 * 1024 * 1024


def rows_of(ref, start, count, stride):
    return ref[pl.ds(start, count, stride=stride), :]


def spread(values):
    return jnp.broadcast_to(values, (SEGS, LANES))


def columns(group):
    return pl.ds(pl.multiple_of(group * LANES, LANES), LANES)


def fetch(hbm, buf, sem, group):
    return pltpu.make_async_copy(hbm.at[:, columns(group)], buf.at[group], sem.at[group])


def order(natural, ordered, values, seg_len):
    for s in range(SEGS):
        natural[pl.ds(s * PITCH, seg_len), :] = values[s * seg_len : (s + 1) * seg_len]
    for q in range(seg_len):
        ordered[q] = rows_of(natural, q, SEGS, PITCH)


def span_kernel(
    x_hbm, o_hbm, g_hbm, rate_hbm, res_hbm, gain_hbm,
    hl_ref, al_ref, hs_ref, as_ref, xq_ref, sq_ref, lam_ref, mu_ref, near_ref, rows_ref, pay_ref,
    x_buf, o_buf, g_buf, rate_buf, res_buf, gain_buf,
    natural, second, rl_t, ends,
    x_sem, o_sem, g_sem, small_sem,
):
    groups, tokens, _ = x_buf.shape
    seg_len = tokens // SEGS
    chunks = seg_len // SUB
    small = [
        pltpu.make_async_copy(hbm, buf, small_sem.at[n])
        for n, (hbm, buf) in enumerate(
            ((rate_hbm, rate_buf), (res_hbm, res_buf), (gain_hbm, gain_buf))
        )
    ]
    for copy in small:
        copy.start()
    for group in range(groups):
        fetch(x_hbm, x_buf, x_sem, group).start()
        fetch(o_hbm, o_buf, o_sem, group).start()
        fetch(g_hbm, g_buf, g_sem, group).start()
    for copy in small:
        copy.wait()
    zero = jnp.zeros((SEGS, LANES), F32)

    def group_step(group, carry):
        cols = columns(group)
        rate = rate_buf[:, cols]
        residue = res_buf[:, cols]
        lam = jnp.exp(-rate)
        mu_rows = jnp.exp(rate * (-float(SUB)))
        big = jnp.exp(rate * (-float(seg_len)))
        rl_rows = residue * lam
        for m in range(MODES):
            lam_ref[group, m] = spread(lam[m : m + 1, :])
            mu_ref[group, m] = spread(mu_rows[m : m + 1, :])
            rl_t[m] = spread(rl_rows[m : m + 1, :])
        rows_ref[0, group] = big
        rows_ref[1, group] = rl_rows
        rows_ref[2, group] = -(rate * residue)
        term = residue
        for d in range(SUB):
            row = jnp.sum(term, axis=0, keepdims=True)
            if d == 0:
                row = row + gain_buf[:, cols]
            near_ref[group, d] = spread(row)
            term = term * lam

        xq = xq_ref.at[group]
        sq = sq_ref.at[group]
        fetch(x_hbm, x_buf, x_sem, group).wait()
        fetch(o_hbm, o_buf, o_sem, group).wait()
        fetch(g_hbm, g_buf, g_sem, group).wait()
        source = x_buf[group].astype(F32)
        signal = g_buf[group].astype(F32) * o_buf[group].astype(F32)
        skip_row = jnp.sum(source * signal, axis=0, keepdims=True)
        order(natural, xq, source, seg_len)
        order(second, sq, signal, seg_len)

        def lag_step(k, acc):
            xs = [xq[k * SUB + j] for j in range(SUB)]
            ss = [sq[k * SUB + j] for j in range(SUB)]
            out = []
            for d in range(SUB):
                total = acc[d]
                for i in range(d, SUB):
                    total = total + ss[i] * xs[i - d]
                out.append(total)
            return tuple(out)

        lagged = lax.fori_loop(0, chunks, lag_step, (zero,) * SUB)
        lag_rows = [jnp.sum(v, axis=0, keepdims=True) for v in lagged]
        res_near = jnp.broadcast_to(lag_rows[0], lam.shape)
        log_near = jnp.zeros_like(lam)
        power = lam
        for d in range(1, SUB):
            term = power * lag_rows[d]
            res_near = res_near + term
            log_near = log_near + float(d) * term
            power = power * lam

        def mode_step(m, carry):
            p1 = lam_ref[group, m]
            mu = mu_ref[group, m]
            rl = rl_t[m]
            p2 = p1 * p1
            p3 = p2 * p1
            p4 = p2 * p2
            pw = [None, p1, p2, p3, p4, p4 * p1, p3 * p3, p4 * p3]
            a_parts = [None] * chunks
            b_parts = [None] * chunks
            for k in reversed(range(chunks)):
                a = sq[k * SUB + SUB - 1] * pw[SUB - 1]
                b = a
                for i in reversed(range(1, SUB - 1)):
                    a = a + sq[k * SUB + i] * pw[i]
                    b = b + a
                a = a + sq[k * SUB]
                a_parts[k] = a
                b_parts[k] = b
                if k == chunks - 1:
                    al_ref[group, k, m] = zero
                    a_run = a
                    b_run = b
                else:
                    al_ref[group, k, m] = rl * a_run
                    b_run = b + mu * (b_run + float(SUB) * a_run)
                    a_run = a + mu * a_run
            for k in range(chunks):
                h = xq[k * SUB] * pw[SUB - 1]
                p = h
                for j in range(1, SUB - 1):
                    h = h + xq[k * SUB + j] * pw[SUB - 1 - j]
                    p = p + h
                h = h + xq[k * SUB + SUB - 1]
                if k == 0:
                    hl_ref[group, k, m] = zero
                    h_run = h
                    p_run = p
                    continue
                hl_ref[group, k, m] = rl * h_run
                res_new = h_run * a_parts[k]
                log_new = p_run * a_parts[k] + h_run * b_parts[k]
                res_x = res_new if k == 1 else res_x + res_new
                log_x = log_new if k == 1 else log_x + log_new
                p_run = p + mu * (p_run + float(SUB) * h_run)
                h_run = h + mu * h_run
            for n, value in enumerate((h_run, p_run, a_run, b_run, res_x, log_x)):
                ends[n, pl.ds(pl.multiple_of(m * SEGS, SEGS), SEGS), :] = value
            return carry

        lax.fori_loop(0, MODES, mode_step, 0)

        def end(n, s):
            return ends[n, pl.ds(s, MODES, stride=SEGS), :]

        span = float(seg_len)
        nothing = jnp.zeros_like(lam)
        h, p, res_x, log_x = nothing, nothing, nothing, nothing
        for s in range(SEGS):
            hs_ref[group, s] = rl_rows * h
            a_s, b_s = end(2, s), end(3, s)
            res_x = res_x + end(4, s) + h * a_s
            log_x = log_x + end(5, s) + (p * a_s + h * b_s)
            p = end(1, s) + big * (p + span * h)
            h = end(0, s) + big * h
        a, b = nothing, nothing
        for s in reversed(range(SEGS)):
            as_ref[group, s] = rl_rows * a
            b = end(3, s) + big * (b + span * a)
            a = end(2, s) + big * a
        res_sum = lam * res_x + res_near
        log_sum = lam * (log_x + res_x) + log_near
        rows = (h, p, a, b, res_sum, log_sum, jnp.broadcast_to(skip_row, lam.shape), rate)
        for n, value in enumerate(rows):
            pay_ref[pl.ds(n * 8 + group, MODES, stride=64), :] = value
        return carry

    lax.fori_loop(0, groups, group_step, 0)


def chain_kernel(tokens, got_ref, back_ref, skip_ref):
    spans = got_ref.shape[0]

    def part(d, n):
        return got_ref[d, pl.ds(8 * n, 8), :]

    rate = part(0, 7)
    lam = jnp.exp(-rate)
    big = jnp.exp(rate * (-float(tokens)))
    span = float(tokens)
    zero = jnp.zeros((8, LANES), F32)
    h, p, res_x, log_x, res_sum, log_sum, skip = (zero,) * 7
    for d in range(spans):
        back_ref[d, pl.ds(0, 8), :] = h
        a_d = part(d, 2)
        res_x = res_x + h * a_d
        log_x = log_x + (p * a_d + h * part(d, 3))
        res_sum = res_sum + part(d, 4)
        log_sum = log_sum + part(d, 5)
        skip = skip + part(d, 6)
        p = part(d, 1) + big * (p + span * h)
        h = part(d, 0) + big * h
    a = zero
    for d in reversed(range(spans)):
        back_ref[d, pl.ds(8, 8), :] = a
        a = part(d, 2) + big * a
    res_total = res_sum + lam * res_x
    log_total = log_sum + lam * (log_x + res_x)
    for d in range(spans):
        back_ref[d, pl.ds(16, 8), :] = res_total
        back_ref[d, pl.ds(24, 8), :] = log_total
    skip_ref[...] = skip


def put(hbm, buf, sem, group):
    return pltpu.make_async_copy(buf.at[group], hbm.at[:, columns(group)], sem.at[group])


def natural_order(natural, seg_len):
    return jnp.concatenate([natural[pl.ds(s * PITCH, seg_len), :] for s in range(SEGS)], axis=0)


def entering(group, first, back_ref, rows_ref, local_ref, run, backward):
    big = rows_ref[0, group]
    state = rows_ref[1, group] * rows_of(back_ref, first + group, MODES, 32)
    for s in reversed(range(SEGS)) if backward else range(SEGS):
        run[pl.ds(s, MODES, stride=SEGS), :] = local_ref[group, s] + state
        if s != (0 if backward else SEGS - 1):
            state = state * big


def far(total, indices, local_ref, group, k, lam_ref, mu_ref, run):
    for m in range(MODES):
        here = pl.ds(m * SEGS, SEGS)
        step = lam_ref[group, m]
        state = run[here, :]
        c = local_ref[group, k, m] + state
        run[here, :] = state * mu_ref[group, m]
        for i in indices:
            total[i] = total[i] + c
            if i != indices[-1]:
                c = c * step


def back_kernel(
    sq_ref, lam_ref, mu_ref, near_ref, rows_ref, al_ref, as_ref, back_ref,
    ig_hbm,
    natural, run, buf, sem,
):
    groups, tokens, _ = buf.shape
    seg_len = tokens // SEGS
    chunks = seg_len // SUB

    def group_step(group, carry):
        entering(group, 8, back_ref, rows_ref, as_ref, run, True)

        def chunk_step(step, carry):
            k = chunks - 1 - step
            near = [near_ref[group, d] for d in range(SUB)]
            ss = [sq_ref[group, k * SUB + j] for j in range(SUB)]
            total = []
            for j in range(SUB):
                value = near[0] * ss[j]
                for d in range(1, SUB - j):
                    value = value + near[d] * ss[j + d]
                total.append(value)
            far(total, list(reversed(range(SUB))), al_ref, group, k, lam_ref, mu_ref, run)
            for j in range(SUB):
                natural[pl.ds(k * SUB + j, SEGS, stride=PITCH), :] = total[j]
            return carry

        lax.fori_loop(0, chunks, chunk_step, 0)
        buf[group] = natural_order(natural, seg_len).astype(jnp.bfloat16)
        put(ig_hbm, buf, sem, group).start()
        return carry

    lax.fori_loop(0, groups, group_step, 0)
    for group in range(groups):
        put(ig_hbm, buf, sem, group).wait()


def gate_kernel(
    g_hbm, xq_ref, lam_ref, mu_ref, near_ref, rows_ref, hl_ref, hs_ref, back_ref,
    gg_hbm,
    natural, run, g_buf, buf, g_sem, sem,
):
    groups, tokens, _ = buf.shape
    seg_len = tokens // SEGS
    chunks = seg_len // SUB
    for group in range(groups):
        fetch(g_hbm, g_buf, g_sem, group).start()

    def group_step(group, carry):
        entering(group, 0, back_ref, rows_ref, hs_ref, run, False)

        def chunk_step(k, carry):
            near = [near_ref[group, d] for d in range(SUB)]
            xs = [xq_ref[group, k * SUB + j] for j in range(SUB)]
            total = []
            for i in range(SUB):
                value = near[0] * xs[i]
                for d in range(1, i + 1):
                    value = value + near[d] * xs[i - d]
                total.append(value)
            far(total, list(range(SUB)), hl_ref, group, k, lam_ref, mu_ref, run)
            for i in range(SUB):
                natural[pl.ds(k * SUB + i, SEGS, stride=PITCH), :] = total[i]
            return carry

        lax.fori_loop(0, chunks, chunk_step, 0)
        fetch(g_hbm, g_buf, g_sem, group).wait()
        mixed = natural_order(natural, seg_len)
        buf[group] = (g_buf[group].astype(F32) * mixed).astype(jnp.bfloat16)
        put(gg_hbm, buf, sem, group).start()
        return carry

    lax.fori_loop(0, groups, group_step, 0)
    for group in range(groups):
        put(gg_hbm, buf, sem, group).wait()


def totals(back_ref, rows_ref, group):
    res_raw = rows_of(back_ref, 16 + group, MODES, 32)
    log_raw = rows_ref[2, group] * rows_of(back_ref, 24 + group, MODES, 32)
    return res_raw, log_raw


def norm_kernel(back_ref, skip_ref, rows_ref, sq_ref):
    groups = skip_ref.shape[0]
    res_sq = jnp.zeros((MODES, LANES), F32)
    log_sq = jnp.zeros((MODES, LANES), F32)
    for group in range(groups):
        res_raw, log_raw = totals(back_ref, rows_ref, group)
        res_sq = res_sq + res_raw * res_raw
        log_sq = log_sq + log_raw * log_raw
    skip = skip_ref[...]
    rows = [jnp.sum(v, axis=0, keepdims=True) for v in (res_sq, log_sq, skip * skip)]
    sq_ref[...] = jnp.concatenate(rows + [jnp.zeros((5, LANES), F32)], axis=0)


def scale_kernel(own_ref, other_ref, back_ref, skip_ref, rows_ref, rg_ref, lg_ref, sg_ref):
    groups = skip_ref.shape[0]
    sums = jnp.sum(own_ref[...] + other_ref[...], axis=1, keepdims=True)

    def factor(n, ceiling):
        return jnp.minimum(1.0, ceiling / jnp.sqrt(sums[n : n + 1, :] + 1e-06))

    limit_modes = math.sqrt(MODES * CHANNELS)
    res_factor = factor(0, limit_modes)
    log_factor = factor(1, limit_modes)
    for group in range(groups):
        cols = pl.ds(group * LANES, LANES)
        res_raw, log_raw = totals(back_ref, rows_ref, group)
        rg_ref[:, cols] = res_raw * res_factor
        lg_ref[:, cols] = log_raw * log_factor
    sg_ref[...] = skip_ref[...] * factor(2, math.sqrt(CHANNELS))


def params():
    return pltpu.CompilerParams(vmem_limit_bytes=VMEM_LIMIT)


def work(ops, moved):
    return pl.CostEstimate(flops=ops, bytes_accessed=moved, transcendentals=0)


HBM = pl.BlockSpec(memory_space=pltpu.HBM)
VMEM = pl.BlockSpec(memory_space=pltpu.VMEM)


def in_hbm(*arrays):
    return [pltpu.with_memory_space_constraint(array, pltpu.HBM) for array in arrays]


def shape(*dims):
    return jax.ShapeDtypeStruct(dims, F32)


def span_call(conv_input, out_gate, grad_out, pole_rate, residue, skip_gain):
    tokens, chan = conv_input.shape
    groups = chan // LANES
    seg_len = tokens // SEGS
    chunks = seg_len // SUB
    wide = pltpu.VMEM((groups, tokens, LANES), jnp.bfloat16)
    natural = pltpu.VMEM((SEGS * PITCH, LANES), F32)
    sems = pltpu.SemaphoreType.DMA((groups,))
    return pl.pallas_call(
        span_kernel,
        in_specs=[HBM] * 6,
        out_specs=[VMEM] * 11,
        out_shape=[
            shape(groups, chunks, MODES, SEGS, LANES),
            shape(groups, chunks, MODES, SEGS, LANES),
            shape(groups, SEGS, MODES, LANES),
            shape(groups, SEGS, MODES, LANES),
            shape(groups, seg_len, SEGS, LANES),
            shape(groups, seg_len, SEGS, LANES),
            shape(groups, MODES, SEGS, LANES),
            shape(groups, MODES, SEGS, LANES),
            shape(groups, SUB, SEGS, LANES),
            shape(3, groups, MODES, LANES),
            shape(MODES * 64, LANES),
        ],
        scratch_shapes=[
            wide, wide, wide,
            pltpu.VMEM((MODES, chan), F32),
            pltpu.VMEM((MODES, chan), F32),
            pltpu.VMEM((1, chan), F32),
            natural, natural,
            pltpu.VMEM((MODES, SEGS, LANES), F32),
            pltpu.VMEM((6, MODES * SEGS, LANES), F32),
            sems, sems, sems, pltpu.SemaphoreType.DMA((3,)),
        ],
        compiler_params=params(),
        name="span",
    )(
        *in_hbm(conv_input, out_gate, grad_out, pole_rate, residue, skip_gain.reshape(1, chan))
    )


def back_call(tokens, chan, sq, lam, mu, near, rows, al, as_, back):
    groups = chan // LANES
    return pl.pallas_call(
        back_kernel,
        in_specs=[VMEM] * 8,
        out_specs=HBM,
        out_shape=jax.ShapeDtypeStruct((tokens, chan), jnp.bfloat16),
        scratch_shapes=[
            pltpu.VMEM((SEGS * PITCH, LANES), F32),
            pltpu.VMEM((MODES * SEGS, LANES), F32),
            pltpu.VMEM((groups, tokens, LANES), jnp.bfloat16),
            pltpu.SemaphoreType.DMA((groups,)),
        ],
        compiler_params=params(),
        cost_estimate=work(40 * MODES * tokens * chan, 16 * tokens * chan),
        name="adjoint",
    )(sq, lam, mu, near, rows, al, as_, back)


def gate_call(grad_out, xq, lam, mu, near, rows, hl, hs, back):
    tokens, chan = grad_out.shape
    groups = chan // LANES
    wide = pltpu.VMEM((groups, tokens, LANES), jnp.bfloat16)
    sems = pltpu.SemaphoreType.DMA((groups,))
    return pl.pallas_call(
        gate_kernel,
        in_specs=[HBM] + [VMEM] * 8,
        out_specs=HBM,
        out_shape=jax.ShapeDtypeStruct((tokens, chan), jnp.bfloat16),
        scratch_shapes=[
            pltpu.VMEM((SEGS * PITCH, LANES), F32),
            pltpu.VMEM((MODES * SEGS, LANES), F32),
            wide, wide, sems, sems,
        ],
        compiler_params=params(),
        cost_estimate=work(40 * MODES * tokens * chan, 16 * tokens * chan),
        name="gate",
    )(*in_hbm(grad_out), xq, lam, mu, near, rows, hl, hs, back)


def outs_call(conv_input, out_gate, grad_out, made, back):
    hl, al, hs, as_, xq, sq, lam, mu, near, rows = made
    tokens, chan = conv_input.shape
    return (
        back_call(tokens, chan, sq, lam, mu, near, rows, al, as_, back),
        gate_call(grad_out, xq, lam, mu, near, rows, hl, hs, back),
    )


def swapped(value, bit):
    peers = lax.axis_size("ch")
    return lax.ppermute(value, "ch", [(i, i ^ bit) for i in range(peers)])


def on_device(conv_input, out_gate, grad_out, pole_rate, residue, skip_gain):
    tokens, chan = conv_input.shape
    groups = chan // LANES
    spans = lax.axis_size("ctx")
    *made, pay = span_call(conv_input, out_gate, grad_out, pole_rate, residue, skip_gain)
    rows = made[9]
    got = lax.all_to_all(pay.reshape(spans, 64, LANES), "ctx", 0, 0)
    back, skip_raw = pl.pallas_call(
        functools.partial(chain_kernel, tokens),
        out_shape=[
            jax.ShapeDtypeStruct((spans, 32, LANES), F32),
            jax.ShapeDtypeStruct((groups, LANES), F32),
        ],
        compiler_params=params(),
        name="chain",
    )(got)
    back = lax.all_to_all(back, "ctx", 0, 0).reshape(MODES * 32, LANES)

    squares = pl.pallas_call(
        norm_kernel,
        out_shape=shape(8, LANES),
        compiler_params=params(),
        name="norm",
    )(back, skip_raw, rows)
    first = swapped(squares, 2)
    input_grad, gate_grad = outs_call(conv_input, out_gate, grad_out, made, back)
    first, input_grad = lax.optimization_barrier((first, input_grad))
    squares = squares + first
    second = swapped(squares, 4)
    second, gate_grad = lax.optimization_barrier((second, gate_grad))
    squares = squares + second
    other = swapped(squares, 1)
    res_out, log_out, skip_out = pl.pallas_call(
        scale_kernel,
        out_shape=[shape(MODES, chan), shape(MODES, chan), shape(groups, LANES)],
        compiler_params=params(),
        name="scale",
    )(squares, other, back, skip_raw, rows)
    return input_grad, gate_grad, res_out, log_out, skip_out.reshape(chan)


def solution(mesh):
    in_specs = (
        P("ctx", "ch"), P("ctx", "ch"), P("ctx", "ch"), P(None, "ch"), P(None, "ch"), P("ch"),
    )
    out_specs = (P("ctx", "ch"), P("ctx", "ch"), P(None, "ch"), P(None, "ch"), P("ch"))
    return jax.shard_map(
        on_device, mesh=mesh, in_specs=in_specs, out_specs=out_specs, check_vma=False
    )
```

```python
import functools
import math

import jax
import jax.numpy as jnp
from jax import lax
from jax.experimental import pallas as pl
from jax.experimental.pallas import tpu as pltpu
from jax.sharding import PartitionSpec as P

CHANNELS = 8192
MODES = 16
LANES = 128
SEGS = 8
SUB = 8
F32 = jnp.float32
AHEAD = 2
END_PITCH = 9
PITCH = 72
VMEM_LIMIT = 16 * 1024 * 1024


def rows_of(ref, start, count, stride):
    return ref[pl.ds(start, count, stride=stride), :]


def spread(values):
    return jnp.broadcast_to(values, (SEGS, LANES))


def columns(group):
    return pl.ds(pl.multiple_of(group * LANES, LANES), LANES)


def span_kernel(
    x_hbm, o_hbm, g_hbm, rate_hbm, res_hbm, gain_hbm,
    hl_ref, al_ref, hs_ref, as_ref, xq_ref, sq_ref, lam_ref, mu_ref, near_ref, rows_ref, pay_ref, g_buf,
    x_buf, o_buf, rate_buf, res_buf, gain_buf,
    natural, second, rl_t, ends,
    x_sem, o_sem, g_sem, small_sem,
):
    tokens = x_buf.shape[1]
    groups = xq_ref.shape[0]
    seg_len = tokens // SEGS
    chunks = seg_len // SUB
    small = [
        pltpu.make_async_copy(hbm, buf, small_sem.at[n])
        for n, (hbm, buf) in enumerate(
            ((rate_hbm, rate_buf), (res_hbm, res_buf), (gain_hbm, gain_buf))
        )
    ]

    def blocks(group, slot):
        return [
            pltpu.make_async_copy(hbm.at[:, columns(group)], buf, sem.at[slot])
            for hbm, buf, sem in (
                (x_hbm, x_buf.at[slot], x_sem),
                (o_hbm, o_buf.at[slot], o_sem),
                (g_hbm, g_buf.at[group], g_sem),
            )
        ]

    for copy in small:
        copy.start()
    for group in range(min(AHEAD, groups)):
        for copy in blocks(group, group):
            copy.start()
    for copy in small:
        copy.wait()
    zero = jnp.zeros((SEGS, LANES), F32)

    def group_step(group, carry):
        slot = lax.rem(group, AHEAD + 1)

        @pl.when(group + AHEAD < groups)
        def _():
            for copy in blocks(group + AHEAD, lax.rem(group + AHEAD, AHEAD + 1)):
                copy.start()

        cols = columns(group)
        rate = rate_buf[:, cols]
        residue = res_buf[:, cols]
        lam = jnp.exp(-rate)
        mu_rows = jnp.exp(rate * (-float(SUB)))
        big = jnp.exp(rate * (-float(seg_len)))
        rl_rows = residue * lam
        for m in range(MODES):
            lam_ref[group, m] = spread(lam[m : m + 1, :])
            mu_ref[group, m] = spread(mu_rows[m : m + 1, :])
            rl_t[m] = spread(rl_rows[m : m + 1, :])
        rows_ref[0, group] = big
        rows_ref[1, group] = rl_rows
        rows_ref[2, group] = -(rate * residue)
        term = residue
        for d in range(SUB):
            row = jnp.sum(term, axis=0, keepdims=True)
            if d == 0:
                row = row + gain_buf[:, cols]
            near_ref[group, d] = spread(row)
            term = term * lam

        xq = xq_ref.at[group]
        sq = sq_ref.at[group]
        for copy in blocks(group, slot):
            copy.wait()
        skip_sum = zero
        for s in range(SEGS):
            part = pl.ds(s * seg_len, seg_len)
            source = x_buf[slot, part, :].astype(F32)
            signal = g_buf[group, part, :].astype(F32) * o_buf[slot, part, :].astype(F32)
            natural[pl.ds(s * PITCH, seg_len), :] = source
            second[pl.ds(s * PITCH, seg_len), :] = signal
            skip_sum = skip_sum + jnp.sum((source * signal).reshape(-1, 8, LANES), axis=0)
        skip_row = jnp.sum(skip_sum, axis=0, keepdims=True)

        def lag_step(k, acc):
            xs = [rows_of(natural, k * SUB + j, SEGS, PITCH) for j in range(SUB)]
            ss = [rows_of(second, k * SUB + j, SEGS, PITCH) for j in range(SUB)]
            for j in range(SUB):
                xq[k * SUB + j] = xs[j]
                sq[k * SUB + j] = ss[j]
            out = []
            for d in range(SUB):
                total = acc[d]
                for i in range(d, SUB):
                    total = total + ss[i] * xs[i - d]
                out.append(total)
            return tuple(out)

        lagged = lax.fori_loop(0, chunks, lag_step, (zero,) * SUB, unroll=8)
        lag_rows = [jnp.sum(v, axis=0, keepdims=True) for v in lagged]
        res_near = jnp.broadcast_to(lag_rows[0], lam.shape)
        log_near = jnp.zeros_like(lam)
        power = lam
        for d in range(1, SUB):
            term = power * lag_rows[d]
            res_near = res_near + term
            log_near = log_near + float(d) * term
            power = power * lam

        def mode_step(m, carry):
            p1 = lam_ref[group, m]
            mu = mu_ref[group, m]
            rl = rl_t[m]
            p2 = p1 * p1
            p3 = p2 * p1
            p4 = p2 * p2
            pw = [None, p1, p2, p3, p4, p4 * p1, p3 * p3, p4 * p3]
            a_parts = [None] * chunks
            b_parts = [None] * chunks
            for k in reversed(range(chunks)):
                a = sq[k * SUB + SUB - 1] * pw[SUB - 1]
                b = a
                for i in reversed(range(1, SUB - 1)):
                    a = a + sq[k * SUB + i] * pw[i]
                    b = b + a
                a = a + sq[k * SUB]
                a_parts[k] = a
                b_parts[k] = b
                if k == chunks - 1:
                    al_ref[group, k, m] = zero
                    a_run = a
                    b_run = b
                else:
                    al_ref[group, k, m] = rl * a_run
                    b_run = b + mu * (b_run + float(SUB) * a_run)
                    a_run = a + mu * a_run
            for k in range(chunks):
                h = xq[k * SUB] * pw[SUB - 1]
                p = h
                for j in range(1, SUB - 1):
                    h = h + xq[k * SUB + j] * pw[SUB - 1 - j]
                    p = p + h
                h = h + xq[k * SUB + SUB - 1]
                if k == 0:
                    hl_ref[group, k, m] = zero
                    h_run = h
                    p_run = p
                    continue
                hl_ref[group, k, m] = rl * h_run
                res_new = h_run * a_parts[k]
                log_new = p_run * a_parts[k] + h_run * b_parts[k]
                res_x = res_new if k == 1 else res_x + res_new
                log_x = log_new if k == 1 else log_x + log_new
                p_run = p + mu * (p_run + float(SUB) * h_run)
                h_run = h + mu * h_run
            for n, value in enumerate((h_run, p_run, a_run, b_run, res_x, log_x)):
                ends[n, pl.ds(m * END_PITCH, SEGS), :] = value
            return carry

        lax.fori_loop(0, MODES, mode_step, 0, unroll=16)

        def end(n, s):
            return ends[n, pl.ds(s, MODES, stride=END_PITCH), :]

        span = float(seg_len)
        nothing = jnp.zeros_like(lam)
        h, p, res_x, log_x = nothing, nothing, nothing, nothing
        for s in range(SEGS):
            hs_ref[group, s] = rl_rows * h
            a_s, b_s = end(2, s), end(3, s)
            res_x = res_x + end(4, s) + h * a_s
            log_x = log_x + end(5, s) + (p * a_s + h * b_s)
            p = end(1, s) + big * (p + span * h)
            h = end(0, s) + big * h
        a, b = nothing, nothing
        for s in reversed(range(SEGS)):
            as_ref[group, s] = rl_rows * a
            b = end(3, s) + big * (b + span * a)
            a = end(2, s) + big * a
        res_sum = lam * res_x + res_near
        log_sum = lam * (log_x + res_x) + log_near
        rows = (h, p, a, b, res_sum, log_sum, jnp.broadcast_to(skip_row, lam.shape), rate)
        for n, value in enumerate(rows):
            pay_ref[pl.ds(n * 8 + group, MODES, stride=64), :] = value
        return carry

    lax.fori_loop(0, groups, group_step, 0)


def chain_kernel(tokens, got_ref, back_ref, skip_ref):
    spans = got_ref.shape[0]

    def part(d, n):
        return got_ref[d, pl.ds(8 * n, 8), :]

    rate = part(0, 7)
    lam = jnp.exp(-rate)
    big = jnp.exp(rate * (-float(tokens)))
    span = float(tokens)
    zero = jnp.zeros((8, LANES), F32)
    h, p, res_x, log_x, res_sum, log_sum, skip = (zero,) * 7
    for d in range(spans):
        back_ref[d, pl.ds(0, 8), :] = h
        a_d = part(d, 2)
        res_x = res_x + h * a_d
        log_x = log_x + (p * a_d + h * part(d, 3))
        res_sum = res_sum + part(d, 4)
        log_sum = log_sum + part(d, 5)
        skip = skip + part(d, 6)
        p = part(d, 1) + big * (p + span * h)
        h = part(d, 0) + big * h
    a = zero
    for d in reversed(range(spans)):
        back_ref[d, pl.ds(8, 8), :] = a
        a = part(d, 2) + big * a
    res_total = res_sum + lam * res_x
    log_total = log_sum + lam * (log_x + res_x)
    for d in range(spans):
        back_ref[d, pl.ds(16, 8), :] = res_total
        back_ref[d, pl.ds(24, 8), :] = log_total
    skip_ref[...] = skip


def put(hbm, buf, sem, group):
    return pltpu.make_async_copy(buf.at[group], hbm.at[:, columns(group)], sem.at[group])


def natural_order(natural, seg_len):
    return jnp.concatenate([natural[pl.ds(s * PITCH, seg_len), :] for s in range(SEGS)], axis=0)


def entering(group, first, back_ref, rows_ref, local_ref, run, backward):
    big = rows_ref[0, group]
    state = rows_ref[1, group] * rows_of(back_ref, first + group, MODES, 32)
    for s in reversed(range(SEGS)) if backward else range(SEGS):
        run[pl.ds(s, MODES, stride=SEGS), :] = local_ref[group, s] + state
        if s != (0 if backward else SEGS - 1):
            state = state * big


def far(total, indices, local_ref, group, k, lam_ref, mu_ref, run):
    for m in range(MODES):
        here = pl.ds(m * SEGS, SEGS)
        step = lam_ref[group, m]
        state = run[here, :]
        c = local_ref[group, k, m] + state
        run[here, :] = state * mu_ref[group, m]
        for i in indices:
            total[i] = total[i] + c
            if i != indices[-1]:
                c = c * step


def back_kernel(
    sq_ref, lam_ref, mu_ref, near_ref, rows_ref, al_ref, as_ref, back_ref,
    ig_ref,
    natural, run,
):
    groups, tokens, _ = ig_ref.shape
    seg_len = tokens // SEGS
    chunks = seg_len // SUB

    def group_step(group, carry):
        entering(group, 8, back_ref, rows_ref, as_ref, run, True)

        def chunk_step(step, carry):
            k = chunks - 1 - step
            near = [near_ref[group, d] for d in range(SUB)]
            ss = [sq_ref[group, k * SUB + j] for j in range(SUB)]
            total = []
            for j in range(SUB):
                value = near[0] * ss[j]
                for d in range(1, SUB - j):
                    value = value + near[d] * ss[j + d]
                total.append(value)
            far(total, list(reversed(range(SUB))), al_ref, group, k, lam_ref, mu_ref, run)
            for j in range(SUB):
                natural[pl.ds(k * SUB + j, SEGS, stride=PITCH), :] = total[j]
            return carry

        lax.fori_loop(0, chunks, chunk_step, 0, unroll=8)
        ig_ref[group] = natural_order(natural, seg_len).astype(jnp.bfloat16)
        return carry

    lax.fori_loop(0, groups, group_step, 0)


def gate_kernel(
    ig_buf, g_buf, xq_ref, lam_ref, mu_ref, near_ref, rows_ref, hl_ref, hs_ref, back_ref,
    ig_hbm, gg_hbm,
    natural, run, buf, ig_sem, sem,
):
    groups, tokens, _ = buf.shape
    seg_len = tokens // SEGS
    chunks = seg_len // SUB
    for group in range(groups):
        put(ig_hbm, ig_buf, ig_sem, group).start()

    def group_step(group, carry):
        entering(group, 0, back_ref, rows_ref, hs_ref, run, False)

        def chunk_step(k, carry):
            near = [near_ref[group, d] for d in range(SUB)]
            xs = [xq_ref[group, k * SUB + j] for j in range(SUB)]
            total = []
            for i in range(SUB):
                value = near[0] * xs[i]
                for d in range(1, i + 1):
                    value = value + near[d] * xs[i - d]
                total.append(value)
            far(total, list(range(SUB)), hl_ref, group, k, lam_ref, mu_ref, run)
            for i in range(SUB):
                natural[pl.ds(k * SUB + i, SEGS, stride=PITCH), :] = total[i]
            return carry

        lax.fori_loop(0, chunks, chunk_step, 0, unroll=8)
        mixed = natural_order(natural, seg_len)
        buf[group] = (g_buf[group].astype(F32) * mixed).astype(jnp.bfloat16)
        put(gg_hbm, buf, sem, group).start()
        return carry

    lax.fori_loop(0, groups, group_step, 0)
    for group in range(groups):
        put(ig_hbm, ig_buf, ig_sem, group).wait()
        put(gg_hbm, buf, sem, group).wait()


def totals(back_ref, rows_ref, group):
    res_raw = rows_of(back_ref, 16 + group, MODES, 32)
    log_raw = rows_ref[2, group] * rows_of(back_ref, 24 + group, MODES, 32)
    return res_raw, log_raw


def norm_kernel(back_ref, skip_ref, rows_ref, sq_ref):
    groups = skip_ref.shape[0]
    res_sq = jnp.zeros((MODES, LANES), F32)
    log_sq = jnp.zeros((MODES, LANES), F32)
    for group in range(groups):
        res_raw, log_raw = totals(back_ref, rows_ref, group)
        res_sq = res_sq + res_raw * res_raw
        log_sq = log_sq + log_raw * log_raw
    skip = skip_ref[...]
    rows = [jnp.sum(v, axis=0, keepdims=True) for v in (res_sq, log_sq, skip * skip)]
    sq_ref[...] = jnp.concatenate(rows + [jnp.zeros((5, LANES), F32)], axis=0)


def scale_kernel(own_ref, other_ref, back_ref, skip_ref, rows_ref, rg_ref, lg_ref, sg_ref):
    groups = skip_ref.shape[0]
    sums = jnp.sum(own_ref[...] + other_ref[...], axis=1, keepdims=True)

    def factor(n, ceiling):
        return jnp.minimum(1.0, ceiling / jnp.sqrt(sums[n : n + 1, :] + 1e-06))

    limit_modes = math.sqrt(MODES * CHANNELS)
    res_factor = factor(0, limit_modes)
    log_factor = factor(1, limit_modes)
    for group in range(groups):
        cols = pl.ds(group * LANES, LANES)
        res_raw, log_raw = totals(back_ref, rows_ref, group)
        rg_ref[:, cols] = res_raw * res_factor
        lg_ref[:, cols] = log_raw * log_factor
    sg_ref[...] = skip_ref[...] * factor(2, math.sqrt(CHANNELS))


def params():
    return pltpu.CompilerParams(vmem_limit_bytes=VMEM_LIMIT)


def work(ops, moved):
    return pl.CostEstimate(flops=ops, bytes_accessed=moved, transcendentals=0)


HBM = pl.BlockSpec(memory_space=pltpu.HBM)
VMEM = pl.BlockSpec(memory_space=pltpu.VMEM)


def in_hbm(*arrays):
    return [pltpu.with_memory_space_constraint(array, pltpu.HBM) for array in arrays]


def shape(*dims):
    return jax.ShapeDtypeStruct(dims, F32)


def span_call(conv_input, out_gate, grad_out, pole_rate, residue, skip_gain):
    tokens, chan = conv_input.shape
    groups = chan // LANES
    seg_len = tokens // SEGS
    chunks = seg_len // SUB
    wide = pltpu.VMEM((AHEAD + 1, tokens, LANES), jnp.bfloat16)
    natural = pltpu.VMEM((SEGS * PITCH, LANES), F32)
    sems = pltpu.SemaphoreType.DMA((AHEAD + 1,))
    return pl.pallas_call(
        span_kernel,
        in_specs=[HBM] * 6,
        out_specs=[VMEM] * 12,
        out_shape=[
            shape(groups, chunks, MODES, SEGS, LANES),
            shape(groups, chunks, MODES, SEGS, LANES),
            shape(groups, SEGS, MODES, LANES),
            shape(groups, SEGS, MODES, LANES),
            shape(groups, seg_len, SEGS, LANES),
            shape(groups, seg_len, SEGS, LANES),
            shape(groups, MODES, SEGS, LANES),
            shape(groups, MODES, SEGS, LANES),
            shape(groups, SUB, SEGS, LANES),
            shape(3, groups, MODES, LANES),
            shape(MODES * 64, LANES),
            jax.ShapeDtypeStruct((groups, tokens, LANES), jnp.bfloat16),
        ],
        scratch_shapes=[
            wide, wide,
            pltpu.VMEM((MODES, chan), F32),
            pltpu.VMEM((MODES, chan), F32),
            pltpu.VMEM((1, chan), F32),
            natural, natural,
            pltpu.VMEM((MODES, SEGS, LANES), F32),
            pltpu.VMEM((6, MODES * END_PITCH, LANES), F32),
            sems, sems, sems, pltpu.SemaphoreType.DMA((3,)),
        ],
        compiler_params=params(),
        name="span",
    )(
        *in_hbm(conv_input, out_gate, grad_out, pole_rate, residue, skip_gain.reshape(1, chan))
    )


def back_call(tokens, sq, lam, mu, near, rows, al, as_, back):
    groups = sq.shape[0]
    return pl.pallas_call(
        back_kernel,
        in_specs=[VMEM] * 8,
        out_specs=VMEM,
        out_shape=jax.ShapeDtypeStruct((groups, tokens, LANES), jnp.bfloat16),
        scratch_shapes=[
            pltpu.VMEM((SEGS * PITCH, LANES), F32),
            pltpu.VMEM((MODES * SEGS, LANES), F32),
        ],
        compiler_params=params(),
        cost_estimate=work(40 * MODES * tokens * groups * LANES, 16 * tokens * groups * LANES),
        name="adjoint",
    )(sq, lam, mu, near, rows, al, as_, back)


def gate_call(ig, g, xq, lam, mu, near, rows, hl, hs, back):
    groups, tokens, _ = g.shape
    chan = groups * LANES
    sems = pltpu.SemaphoreType.DMA((groups,))
    return pl.pallas_call(
        gate_kernel,
        in_specs=[VMEM] * 10,
        out_specs=[HBM] * 2,
        out_shape=[jax.ShapeDtypeStruct((tokens, chan), jnp.bfloat16)] * 2,
        scratch_shapes=[
            pltpu.VMEM((SEGS * PITCH, LANES), F32),
            pltpu.VMEM((MODES * SEGS, LANES), F32),
            pltpu.VMEM((groups, tokens, LANES), jnp.bfloat16),
            sems, sems,
        ],
        compiler_params=params(),
        cost_estimate=work(40 * MODES * tokens * chan, 16 * tokens * chan),
        name="gate",
    )(ig, g, xq, lam, mu, near, rows, hl, hs, back)


def swapped(value, bit):
    peers = lax.axis_size("ch")
    return lax.ppermute(value, "ch", [(i, i ^ bit) for i in range(peers)])


def on_device(conv_input, out_gate, grad_out, pole_rate, residue, skip_gain):
    tokens, chan = conv_input.shape
    groups = chan // LANES
    spans = lax.axis_size("ctx")
    hl, al, hs, as_, xq, sq, lam, mu, near, rows, pay, g = span_call(
        conv_input, out_gate, grad_out, pole_rate, residue, skip_gain
    )
    got = lax.all_to_all(pay.reshape(spans, 64, LANES), "ctx", 0, 0)
    back, skip_raw = pl.pallas_call(
        functools.partial(chain_kernel, tokens),
        out_shape=[shape(spans, 32, LANES), shape(groups, LANES)],
        compiler_params=params(),
        name="chain",
    )(got)
    back = lax.all_to_all(back, "ctx", 0, 0).reshape(MODES * 32, LANES)

    squares = pl.pallas_call(
        norm_kernel,
        out_shape=shape(8, LANES),
        compiler_params=params(),
        name="norm",
    )(back, skip_raw, rows)
    first = swapped(squares, 2)
    ig = back_call(tokens, sq, lam, mu, near, rows, al, as_, back)
    first, ig = lax.optimization_barrier((first, ig))
    squares = squares + first
    second = swapped(squares, 4)
    input_grad, gate_grad = gate_call(ig, g, xq, lam, mu, near, rows, hl, hs, back)
    second, input_grad, gate_grad = lax.optimization_barrier((second, input_grad, gate_grad))
    squares = squares + second
    other = swapped(squares, 1)
    res_out, log_out, skip_out = pl.pallas_call(
        scale_kernel,
        out_shape=[shape(MODES, chan), shape(MODES, chan), shape(groups, LANES)],
        compiler_params=params(),
        name="scale",
    )(squares, other, back, skip_raw, rows)
    return input_grad, gate_grad, res_out, log_out, skip_out.reshape(chan)


def solution(mesh):
    in_specs = (
        P("ctx", "ch"), P("ctx", "ch"), P("ctx", "ch"), P(None, "ch"), P(None, "ch"), P("ch"),
    )
    out_specs = (P("ctx", "ch"), P("ctx", "ch"), P(None, "ch"), P(None, "ch"), P("ch"))
    return jax.shard_map(
        on_device, mesh=mesh, in_specs=in_specs, out_specs=out_specs, check_vma=False
    )
```

```python
import functools
import math

import jax
import jax.numpy as jnp
from jax import lax
from jax.experimental import pallas as pl
from jax.experimental.pallas import tpu as pltpu
from jax.sharding import PartitionSpec as P

CHANNELS = 8192
MODES = 16
LANES = 128
SEGS = 8
SUB = 8
F32 = jnp.float32
AHEAD = 2
END_PITCH = 9
SENT = 48
BACK = 40
PITCH = 72
VMEM_LIMIT = 16 * 1024 * 1024


def rows_of(ref, start, count, stride):
    return ref[pl.ds(start, count, stride=stride), :]


def spread(values):
    return jnp.broadcast_to(values, (SEGS, LANES))


def columns(group):
    return pl.ds(pl.multiple_of(group * LANES, LANES), LANES)


def span_kernel(
    x_hbm, o_hbm, g_hbm, rate_hbm, res_hbm, gain_hbm,
    hl_ref, al_ref, hs_ref, as_ref, xq_ref, sq_ref, lam_ref, mu_ref, near_ref, rows_ref, skip_ref, pay_ref, g_buf,
    x_buf, o_buf, rate_buf, res_buf, gain_buf,
    natural, second, rl_t, ends,
    x_sem, o_sem, g_sem, small_sem,
):
    tokens = x_buf.shape[1]
    groups = xq_ref.shape[0]
    seg_len = tokens // SEGS
    chunks = seg_len // SUB
    small = [
        pltpu.make_async_copy(hbm, buf, small_sem.at[n])
        for n, (hbm, buf) in enumerate(
            ((rate_hbm, rate_buf), (res_hbm, res_buf), (gain_hbm, gain_buf))
        )
    ]

    def blocks(group, slot):
        return [
            pltpu.make_async_copy(hbm.at[:, columns(group)], buf, sem.at[slot])
            for hbm, buf, sem in (
                (x_hbm, x_buf.at[slot], x_sem),
                (o_hbm, o_buf.at[slot], o_sem),
                (g_hbm, g_buf.at[group], g_sem),
            )
        ]

    for copy in small:
        copy.start()
    for group in range(min(AHEAD, groups)):
        for copy in blocks(group, group):
            copy.start()
    for copy in small:
        copy.wait()
    zero = jnp.zeros((SEGS, LANES), F32)

    def group_step(group, carry):
        slot = lax.rem(group, AHEAD + 1)

        @pl.when(group + AHEAD < groups)
        def _():
            for copy in blocks(group + AHEAD, lax.rem(group + AHEAD, AHEAD + 1)):
                copy.start()

        cols = columns(group)
        rate = rate_buf[:, cols]
        residue = res_buf[:, cols]
        lam = jnp.exp(-rate)
        mu_rows = jnp.exp(rate * (-float(SUB)))
        big = jnp.exp(rate * (-float(seg_len)))
        rl_rows = residue * lam
        for m in range(MODES):
            lam_ref[group, m] = spread(lam[m : m + 1, :])
            mu_ref[group, m] = spread(mu_rows[m : m + 1, :])
            rl_t[m] = spread(rl_rows[m : m + 1, :])
        rows_ref[0, group] = big
        rows_ref[1, group] = rl_rows
        rows_ref[2, group] = -(rate * residue)
        rows_ref[3, group] = rate
        term = residue
        for d in range(SUB):
            row = jnp.sum(term, axis=0, keepdims=True)
            if d == 0:
                row = row + gain_buf[:, cols]
            near_ref[group, d] = spread(row)
            term = term * lam

        xq = xq_ref.at[group]
        sq = sq_ref.at[group]
        for copy in blocks(group, slot):
            copy.wait()
        for s in range(SEGS):
            part = pl.ds(s * seg_len, seg_len)
            source = x_buf[slot, part, :].astype(F32)
            signal = g_buf[group, part, :].astype(F32) * o_buf[slot, part, :].astype(F32)
            natural[pl.ds(s * PITCH, seg_len), :] = source
            second[pl.ds(s * PITCH, seg_len), :] = signal

        def lag_step(k, acc):
            xs = [rows_of(natural, k * SUB + j, SEGS, PITCH) for j in range(SUB)]
            ss = [rows_of(second, k * SUB + j, SEGS, PITCH) for j in range(SUB)]
            for j in range(SUB):
                xq[k * SUB + j] = xs[j]
                sq[k * SUB + j] = ss[j]
            out = []
            for d in range(SUB):
                total = acc[d]
                for i in range(d, SUB):
                    total = total + ss[i] * xs[i - d]
                out.append(total)
            return tuple(out)

        lagged = lax.fori_loop(0, chunks, lag_step, (zero,) * SUB, unroll=8)
        lag_rows = [jnp.sum(v, axis=0, keepdims=True) for v in lagged]
        skip_ref[pl.ds(group, 1), :] = lag_rows[0]
        res_near = jnp.broadcast_to(lag_rows[0], lam.shape)
        log_near = jnp.zeros_like(lam)
        power = lam
        for d in range(1, SUB):
            term = power * lag_rows[d]
            res_near = res_near + term
            log_near = log_near + float(d) * term
            power = power * lam

        def mode_step(m, carry):
            p1 = lam_ref[group, m]
            mu = mu_ref[group, m]
            rl = rl_t[m]
            p2 = p1 * p1
            p3 = p2 * p1
            p4 = p2 * p2
            pw = [None, p1, p2, p3, p4, p4 * p1, p3 * p3, p4 * p3]
            a_parts = [None] * chunks
            b_parts = [None] * chunks
            for k in reversed(range(chunks)):
                a = sq[k * SUB + SUB - 1] * pw[SUB - 1]
                b = a
                for i in reversed(range(1, SUB - 1)):
                    a = a + sq[k * SUB + i] * pw[i]
                    b = b + a
                a = a + sq[k * SUB]
                a_parts[k] = a
                b_parts[k] = b
                if k == chunks - 1:
                    al_ref[group, k, m] = zero
                    a_run = a
                    b_run = b
                else:
                    al_ref[group, k, m] = rl * a_run
                    b_run = b + mu * (b_run + float(SUB) * a_run)
                    a_run = a + mu * a_run
            for k in range(chunks):
                h = xq[k * SUB] * pw[SUB - 1]
                p = h
                for j in range(1, SUB - 1):
                    h = h + xq[k * SUB + j] * pw[SUB - 1 - j]
                    p = p + h
                h = h + xq[k * SUB + SUB - 1]
                if k == 0:
                    hl_ref[group, k, m] = zero
                    h_run = h
                    p_run = p
                    continue
                hl_ref[group, k, m] = rl * h_run
                res_new = h_run * a_parts[k]
                log_new = p_run * a_parts[k] + h_run * b_parts[k]
                res_x = res_new if k == 1 else res_x + res_new
                log_x = log_new if k == 1 else log_x + log_new
                p_run = p + mu * (p_run + float(SUB) * h_run)
                h_run = h + mu * h_run
            for n, value in enumerate((h_run, p_run, a_run, b_run, res_x, log_x)):
                ends[n, pl.ds(m * END_PITCH, SEGS), :] = value
            return carry

        lax.fori_loop(0, MODES, mode_step, 0, unroll=16)

        def end(n, s):
            return ends[n, pl.ds(s, MODES, stride=END_PITCH), :]

        span = float(seg_len)
        nothing = jnp.zeros_like(lam)
        h, p, res_x, log_x = nothing, nothing, nothing, nothing
        for s in range(SEGS):
            hs_ref[group, s] = rl_rows * h
            a_s, b_s = end(2, s), end(3, s)
            res_x = res_x + end(4, s) + h * a_s
            log_x = log_x + end(5, s) + (p * a_s + h * b_s)
            p = end(1, s) + big * (p + span * h)
            h = end(0, s) + big * h
        a, b = nothing, nothing
        for s in reversed(range(SEGS)):
            as_ref[group, s] = rl_rows * a
            b = end(3, s) + big * (b + span * a)
            a = end(2, s) + big * a
        res_sum = lam * res_x + res_near
        log_sum = lam * (log_x + res_x) + log_near
        rows = (h, p, a, b, res_sum, log_sum)
        for n, value in enumerate(rows):
            pay_ref[pl.ds(n * 8 + group, MODES, stride=SENT), :] = value
        return carry

    lax.fori_loop(0, groups, group_step, 0)


def chain_kernel(tokens, got_ref, rows_ref, skip_ref, back_ref):
    spans = got_ref.shape[0]
    groups = skip_ref.shape[0]
    own = lax.axis_index("ctx")

    def part(d, n):
        return got_ref[d, pl.ds(8 * n, 8), :]

    rate = jnp.concatenate(
        [rows_ref[3, group, pl.ds(own, 1), :] for group in range(groups)], axis=0
    )
    lam = jnp.exp(-rate)
    big = jnp.exp(rate * (-float(tokens)))
    span = float(tokens)
    zero = jnp.zeros((8, LANES), F32)
    h, p, res_x, log_x, res_sum, log_sum = (zero,) * 6
    for d in range(spans):
        back_ref[d, pl.ds(0, 8), :] = h
        a_d = part(d, 2)
        res_x = res_x + h * a_d
        log_x = log_x + (p * a_d + h * part(d, 3))
        res_sum = res_sum + part(d, 4)
        log_sum = log_sum + part(d, 5)
        p = part(d, 1) + big * (p + span * h)
        h = part(d, 0) + big * h
    a = zero
    for d in reversed(range(spans)):
        back_ref[d, pl.ds(8, 8), :] = a
        a = part(d, 2) + big * a
    res_total = res_sum + lam * res_x
    log_total = log_sum + lam * (log_x + res_x)
    for d in range(spans):
        back_ref[d, pl.ds(16, 8), :] = res_total
        back_ref[d, pl.ds(24, 8), :] = log_total
        back_ref[d, pl.ds(32, 8), :] = skip_ref[...]


def put(hbm, buf, sem, group):
    return pltpu.make_async_copy(buf.at[group], hbm.at[:, columns(group)], sem.at[group])


def natural_order(natural, seg_len):
    return jnp.concatenate([natural[pl.ds(s * PITCH, seg_len), :] for s in range(SEGS)], axis=0)


def entering(group, first, back_ref, rows_ref, local_ref, run, backward):
    big = rows_ref[0, group]
    state = rows_ref[1, group] * rows_of(back_ref, first + group, MODES, BACK)
    for s in reversed(range(SEGS)) if backward else range(SEGS):
        run[pl.ds(s, MODES, stride=SEGS), :] = local_ref[group, s] + state
        if s != (0 if backward else SEGS - 1):
            state = state * big


def far(total, indices, local_ref, group, k, lam_ref, mu_ref, run):
    for m in range(MODES):
        here = pl.ds(m * SEGS, SEGS)
        step = lam_ref[group, m]
        state = run[here, :]
        c = local_ref[group, k, m] + state
        run[here, :] = state * mu_ref[group, m]
        for i in indices:
            total[i] = total[i] + c
            if i != indices[-1]:
                c = c * step


def back_kernel(
    sq_ref, lam_ref, mu_ref, near_ref, rows_ref, al_ref, as_ref, back_ref,
    ig_ref,
    natural, run,
):
    groups, tokens, _ = ig_ref.shape
    seg_len = tokens // SEGS
    chunks = seg_len // SUB

    def group_step(group, carry):
        entering(group, 8, back_ref, rows_ref, as_ref, run, True)

        def chunk_step(step, carry):
            k = chunks - 1 - step
            near = [near_ref[group, d] for d in range(SUB)]
            ss = [sq_ref[group, k * SUB + j] for j in range(SUB)]
            total = []
            for j in range(SUB):
                value = near[0] * ss[j]
                for d in range(1, SUB - j):
                    value = value + near[d] * ss[j + d]
                total.append(value)
            far(total, list(reversed(range(SUB))), al_ref, group, k, lam_ref, mu_ref, run)
            for j in range(SUB):
                natural[pl.ds(k * SUB + j, SEGS, stride=PITCH), :] = total[j]
            return carry

        lax.fori_loop(0, chunks, chunk_step, 0, unroll=8)
        ig_ref[group] = natural_order(natural, seg_len).astype(jnp.bfloat16)
        return carry

    lax.fori_loop(0, groups, group_step, 0)


def gate_kernel(
    ig_buf, g_buf, xq_ref, lam_ref, mu_ref, near_ref, rows_ref, hl_ref, hs_ref, back_ref,
    ig_hbm, gg_hbm,
    natural, run, buf, ig_sem, sem,
):
    groups, tokens, _ = buf.shape
    seg_len = tokens // SEGS
    chunks = seg_len // SUB
    for group in range(groups):
        put(ig_hbm, ig_buf, ig_sem, group).start()

    def group_step(group, carry):
        entering(group, 0, back_ref, rows_ref, hs_ref, run, False)

        def chunk_step(k, carry):
            near = [near_ref[group, d] for d in range(SUB)]
            xs = [xq_ref[group, k * SUB + j] for j in range(SUB)]
            total = []
            for i in range(SUB):
                value = near[0] * xs[i]
                for d in range(1, i + 1):
                    value = value + near[d] * xs[i - d]
                total.append(value)
            far(total, list(range(SUB)), hl_ref, group, k, lam_ref, mu_ref, run)
            for i in range(SUB):
                natural[pl.ds(k * SUB + i, SEGS, stride=PITCH), :] = total[i]
            return carry

        lax.fori_loop(0, chunks, chunk_step, 0, unroll=8)
        mixed = natural_order(natural, seg_len)
        buf[group] = (g_buf[group].astype(F32) * mixed).astype(jnp.bfloat16)
        put(gg_hbm, buf, sem, group).start()
        return carry

    lax.fori_loop(0, groups, group_step, 0)
    for group in range(groups):
        put(ig_hbm, ig_buf, ig_sem, group).wait()
        put(gg_hbm, buf, sem, group).wait()


def totals(back_ref, rows_ref, group):
    res_raw = rows_of(back_ref, 16 + group, MODES, BACK)
    log_raw = rows_ref[2, group] * rows_of(back_ref, 24 + group, MODES, BACK)
    return res_raw, log_raw


def skip_total(back_ref):
    total = back_ref[pl.ds(32, 8), :]
    for span in range(1, back_ref.shape[0] // BACK):
        total = total + back_ref[pl.ds(span * BACK + 32, 8), :]
    return total


def norm_kernel(back_ref, rows_ref, sq_ref):
    groups = rows_ref.shape[1]
    res_sq = jnp.zeros((MODES, LANES), F32)
    log_sq = jnp.zeros((MODES, LANES), F32)
    for group in range(groups):
        res_raw, log_raw = totals(back_ref, rows_ref, group)
        res_sq = res_sq + res_raw * res_raw
        log_sq = log_sq + log_raw * log_raw
    skip = skip_total(back_ref)
    rows = [jnp.sum(v, axis=0, keepdims=True) for v in (res_sq, log_sq, skip * skip)]
    sq_ref[...] = jnp.concatenate(rows + [jnp.zeros((5, LANES), F32)], axis=0)


def scale_kernel(own_ref, other_ref, back_ref, rows_ref, rg_ref, lg_ref, sg_ref):
    groups = rows_ref.shape[1]
    sums = jnp.sum(own_ref[...] + other_ref[...], axis=1, keepdims=True)

    def factor(n, ceiling):
        return jnp.minimum(1.0, ceiling / jnp.sqrt(sums[n : n + 1, :] + 1e-06))

    limit_modes = math.sqrt(MODES * CHANNELS)
    res_factor = factor(0, limit_modes)
    log_factor = factor(1, limit_modes)
    for group in range(groups):
        cols = pl.ds(group * LANES, LANES)
        res_raw, log_raw = totals(back_ref, rows_ref, group)
        rg_ref[:, cols] = res_raw * res_factor
        lg_ref[:, cols] = log_raw * log_factor
    sg_ref[...] = skip_total(back_ref) * factor(2, math.sqrt(CHANNELS))


def params():
    return pltpu.CompilerParams(vmem_limit_bytes=VMEM_LIMIT)


def work(ops, moved):
    return pl.CostEstimate(flops=ops, bytes_accessed=moved, transcendentals=0)


HBM = pl.BlockSpec(memory_space=pltpu.HBM)
VMEM = pl.BlockSpec(memory_space=pltpu.VMEM)


def in_hbm(*arrays):
    return [pltpu.with_memory_space_constraint(array, pltpu.HBM) for array in arrays]


def shape(*dims):
    return jax.ShapeDtypeStruct(dims, F32)


def span_call(conv_input, out_gate, grad_out, pole_rate, residue, skip_gain):
    tokens, chan = conv_input.shape
    groups = chan // LANES
    seg_len = tokens // SEGS
    chunks = seg_len // SUB
    wide = pltpu.VMEM((AHEAD + 1, tokens, LANES), jnp.bfloat16)
    natural = pltpu.VMEM((SEGS * PITCH, LANES), F32)
    sems = pltpu.SemaphoreType.DMA((AHEAD + 1,))
    return pl.pallas_call(
        span_kernel,
        in_specs=[HBM] * 6,
        out_specs=[VMEM] * 13,
        out_shape=[
            shape(groups, chunks, MODES, SEGS, LANES),
            shape(groups, chunks, MODES, SEGS, LANES),
            shape(groups, SEGS, MODES, LANES),
            shape(groups, SEGS, MODES, LANES),
            shape(groups, seg_len, SEGS, LANES),
            shape(groups, seg_len, SEGS, LANES),
            shape(groups, MODES, SEGS, LANES),
            shape(groups, MODES, SEGS, LANES),
            shape(groups, SUB, SEGS, LANES),
            shape(4, groups, MODES, LANES),
            shape(groups, LANES),
            shape(MODES * SENT, LANES),
            jax.ShapeDtypeStruct((groups, tokens, LANES), jnp.bfloat16),
        ],
        scratch_shapes=[
            wide, wide,
            pltpu.VMEM((MODES, chan), F32),
            pltpu.VMEM((MODES, chan), F32),
            pltpu.VMEM((1, chan), F32),
            natural, natural,
            pltpu.VMEM((MODES, SEGS, LANES), F32),
            pltpu.VMEM((6, MODES * END_PITCH, LANES), F32),
            sems, sems, sems, pltpu.SemaphoreType.DMA((3,)),
        ],
        compiler_params=params(),
        name="span",
    )(
        *in_hbm(conv_input, out_gate, grad_out, pole_rate, residue, skip_gain.reshape(1, chan))
    )


def back_call(tokens, sq, lam, mu, near, rows, al, as_, back):
    groups = sq.shape[0]
    return pl.pallas_call(
        back_kernel,
        in_specs=[VMEM] * 8,
        out_specs=VMEM,
        out_shape=jax.ShapeDtypeStruct((groups, tokens, LANES), jnp.bfloat16),
        scratch_shapes=[
            pltpu.VMEM((SEGS * PITCH, LANES), F32),
            pltpu.VMEM((MODES * SEGS, LANES), F32),
        ],
        compiler_params=params(),
        cost_estimate=work(40 * MODES * tokens * groups * LANES, 16 * tokens * groups * LANES),
        name="adjoint",
    )(sq, lam, mu, near, rows, al, as_, back)


def gate_call(ig, g, xq, lam, mu, near, rows, hl, hs, back):
    groups, tokens, _ = g.shape
    chan = groups * LANES
    sems = pltpu.SemaphoreType.DMA((groups,))
    return pl.pallas_call(
        gate_kernel,
        in_specs=[VMEM] * 10,
        out_specs=[HBM] * 2,
        out_shape=[jax.ShapeDtypeStruct((tokens, chan), jnp.bfloat16)] * 2,
        scratch_shapes=[
            pltpu.VMEM((SEGS * PITCH, LANES), F32),
            pltpu.VMEM((MODES * SEGS, LANES), F32),
            pltpu.VMEM((groups, tokens, LANES), jnp.bfloat16),
            sems, sems,
        ],
        compiler_params=params(),
        cost_estimate=work(40 * MODES * tokens * chan, 16 * tokens * chan),
        name="gate",
    )(ig, g, xq, lam, mu, near, rows, hl, hs, back)


def swapped(value, bit):
    peers = lax.axis_size("ch")
    return lax.ppermute(value, "ch", [(i, i ^ bit) for i in range(peers)])


def on_device(conv_input, out_gate, grad_out, pole_rate, residue, skip_gain):
    tokens, chan = conv_input.shape
    groups = chan // LANES
    spans = lax.axis_size("ctx")
    hl, al, hs, as_, xq, sq, lam, mu, near, rows, skip, pay, g = span_call(
        conv_input, out_gate, grad_out, pole_rate, residue, skip_gain
    )
    got = lax.all_to_all(pay.reshape(spans, SENT, LANES), "ctx", 0, 0)
    back = pl.pallas_call(
        functools.partial(chain_kernel, tokens),
        out_shape=shape(spans, BACK, LANES),
        compiler_params=params(),
        name="chain",
    )(got, rows, skip)
    back = lax.all_to_all(back, "ctx", 0, 0).reshape(MODES * BACK, LANES)

    squares = pl.pallas_call(
        norm_kernel,
        out_shape=shape(8, LANES),
        compiler_params=params(),
        name="norm",
    )(back, rows)
    first = swapped(squares, 2)
    ig = back_call(tokens, sq, lam, mu, near, rows, al, as_, back)
    first, ig = lax.optimization_barrier((first, ig))
    squares = squares + first
    second = swapped(squares, 4)
    input_grad, gate_grad = gate_call(ig, g, xq, lam, mu, near, rows, hl, hs, back)
    second, input_grad, gate_grad = lax.optimization_barrier((second, input_grad, gate_grad))
    squares = squares + second
    other = swapped(squares, 1)
    res_out, log_out, skip_out = pl.pallas_call(
        scale_kernel,
        out_shape=[shape(MODES, chan), shape(MODES, chan), shape(groups, LANES)],
        compiler_params=params(),
        name="scale",
    )(squares, other, back, rows)
    return input_grad, gate_grad, res_out, log_out, skip_out.reshape(chan)


def solution(mesh):
    in_specs = (
        P("ctx", "ch"), P("ctx", "ch"), P("ctx", "ch"), P(None, "ch"), P(None, "ch"), P("ch"),
    )
    out_specs = (P("ctx", "ch"), P("ctx", "ch"), P(None, "ch"), P(None, "ch"), P("ch"))
    return jax.shard_map(
        on_device, mesh=mesh, in_specs=in_specs, out_specs=out_specs, check_vma=False
    )
```

```python
import functools
import math

import jax
import jax.numpy as jnp
from jax import lax
from jax.experimental import pallas as pl
from jax.experimental.pallas import tpu as pltpu
from jax.sharding import PartitionSpec as P

CHANNELS = 8192
MODES = 16
LANES = 128
SEGS = 8
SUB = 8
F32 = jnp.float32
LATE = 2
AHEAD = 2
END_PITCH = 9
SENT = 48
BACK = 40
PITCH = 72
VMEM_LIMIT = 16 * 1024 * 1024


def rows_of(ref, start, count, stride):
    return ref[pl.ds(start, count, stride=stride), :]


def spread(values):
    return jnp.broadcast_to(values, (SEGS, LANES))


def columns(group):
    return pl.ds(pl.multiple_of(group * LANES, LANES), LANES)


def span_kernel(
    x_hbm, o_hbm, g_hbm, rate_hbm, res_hbm, gain_hbm,
    hl_ref, al_ref, hs_ref, as_ref, xq_ref, sq_ref, lam_ref, mu_ref, near_ref, rows_ref, skip_ref, pay_ref, g_buf,
    x_buf, o_buf, rate_buf, res_buf, gain_buf,
    natural, second, rl_t, ends,
    x_sem, o_sem, g_sem, small_sem,
):
    tokens = x_buf.shape[1]
    groups = xq_ref.shape[0]
    seg_len = tokens // SEGS
    chunks = seg_len // SUB
    small = [
        pltpu.make_async_copy(hbm, buf, small_sem.at[n])
        for n, (hbm, buf) in enumerate(
            ((rate_hbm, rate_buf), (res_hbm, res_buf), (gain_hbm, gain_buf))
        )
    ]

    def blocks(group, slot):
        return [
            pltpu.make_async_copy(hbm.at[:, columns(group)], buf, sem.at[slot])
            for hbm, buf, sem in (
                (x_hbm, x_buf.at[slot], x_sem),
                (o_hbm, o_buf.at[slot], o_sem),
                (g_hbm, g_buf.at[group], g_sem),
            )
        ]

    for copy in blocks(0, 0) + small:
        copy.start()
    for group in range(1, min(AHEAD, groups)):
        for copy in blocks(group, group):
            copy.start()
    for copy in small:
        copy.wait()
    zero = jnp.zeros((SEGS, LANES), F32)

    def group_step(group, carry):
        slot = lax.rem(group, AHEAD + 1)

        @pl.when(group + AHEAD < groups)
        def _():
            for copy in blocks(group + AHEAD, lax.rem(group + AHEAD, AHEAD + 1)):
                copy.start()

        cols = columns(group)
        rate = rate_buf[:, cols]
        residue = res_buf[:, cols]
        lam = jnp.exp(-rate)
        mu_rows = jnp.exp(rate * (-float(SUB)))
        big = jnp.exp(rate * (-float(seg_len)))
        rl_rows = residue * lam
        for m in range(MODES):
            lam_ref[group, m] = spread(lam[m : m + 1, :])
            mu_ref[group, m] = spread(mu_rows[m : m + 1, :])
            rl_t[m] = spread(rl_rows[m : m + 1, :])
        rows_ref[0, group] = big
        rows_ref[1, group] = rl_rows
        rows_ref[2, group] = -(rate * residue)
        rows_ref[3, group] = rate
        term = residue
        for d in range(SUB):
            row = jnp.sum(term, axis=0, keepdims=True)
            if d == 0:
                row = row + gain_buf[:, cols]
            near_ref[group, d] = spread(row)
            term = term * lam

        xq = xq_ref.at[group]
        sq = sq_ref.at[group]
        for copy in blocks(group, slot):
            copy.wait()
        for s in range(SEGS):
            part = pl.ds(s * seg_len, seg_len)
            source = x_buf[slot, part, :].astype(F32)
            signal = g_buf[group, part, :].astype(F32) * o_buf[slot, part, :].astype(F32)
            natural[pl.ds(s * PITCH, seg_len), :] = source
            second[pl.ds(s * PITCH, seg_len), :] = signal

        def lag_step(k, acc):
            xs = [rows_of(natural, k * SUB + j, SEGS, PITCH) for j in range(SUB)]
            ss = [rows_of(second, k * SUB + j, SEGS, PITCH) for j in range(SUB)]
            for j in range(SUB):
                xq[k * SUB + j] = xs[j]
                sq[k * SUB + j] = ss[j]
            out = []
            for d in range(SUB):
                total = acc[d]
                for i in range(d, SUB):
                    total = total + ss[i] * xs[i - d]
                out.append(total)
            return tuple(out)

        lagged = lax.fori_loop(0, chunks, lag_step, (zero,) * SUB, unroll=8)
        lag_rows = [jnp.sum(v, axis=0, keepdims=True) for v in lagged]
        skip_ref[pl.ds(group, 1), :] = lag_rows[0]
        res_near = jnp.broadcast_to(lag_rows[0], lam.shape)
        log_near = jnp.zeros_like(lam)
        power = lam
        for d in range(1, SUB):
            term = power * lag_rows[d]
            res_near = res_near + term
            log_near = log_near + float(d) * term
            power = power * lam

        def mode_step(m, carry):
            p1 = lam_ref[group, m]
            mu = mu_ref[group, m]
            rl = rl_t[m]
            p2 = p1 * p1
            p3 = p2 * p1
            p4 = p2 * p2
            pw = [None, p1, p2, p3, p4, p4 * p1, p3 * p3, p4 * p3]
            a_parts = [None] * chunks
            b_parts = [None] * chunks
            for k in reversed(range(chunks)):
                a = sq[k * SUB + SUB - 1] * pw[SUB - 1]
                b = a
                for i in reversed(range(1, SUB - 1)):
                    a = a + sq[k * SUB + i] * pw[i]
                    b = b + a
                a = a + sq[k * SUB]
                a_parts[k] = a
                b_parts[k] = b
                if k == chunks - 1:
                    al_ref[group, k, m] = zero
                    a_run = a
                    b_run = b
                else:
                    al_ref[group, k, m] = rl * a_run
                    b_run = b + mu * (b_run + float(SUB) * a_run)
                    a_run = a + mu * a_run
            for k in range(chunks):
                h = xq[k * SUB] * pw[SUB - 1]
                p = h
                for j in range(1, SUB - 1):
                    h = h + xq[k * SUB + j] * pw[SUB - 1 - j]
                    p = p + h
                h = h + xq[k * SUB + SUB - 1]
                if k == 0:
                    hl_ref[group, k, m] = zero
                    h_run = h
                    p_run = p
                    continue
                hl_ref[group, k, m] = rl * h_run
                res_new = h_run * a_parts[k]
                log_new = p_run * a_parts[k] + h_run * b_parts[k]
                res_x = res_new if k == 1 else res_x + res_new
                log_x = log_new if k == 1 else log_x + log_new
                p_run = p + mu * (p_run + float(SUB) * h_run)
                h_run = h + mu * h_run
            for n, value in enumerate((h_run, p_run, a_run, b_run, res_x, log_x)):
                ends[n, pl.ds(m * END_PITCH, SEGS), :] = value
            return carry

        lax.fori_loop(0, MODES, mode_step, 0, unroll=16)

        def end(n, s):
            return ends[n, pl.ds(s, MODES, stride=END_PITCH), :]

        span = float(seg_len)
        nothing = jnp.zeros_like(lam)
        h, p, res_x, log_x = nothing, nothing, nothing, nothing
        for s in range(SEGS):
            hs_ref[group, s] = rl_rows * h
            a_s, b_s = end(2, s), end(3, s)
            res_x = res_x + end(4, s) + h * a_s
            log_x = log_x + end(5, s) + (p * a_s + h * b_s)
            p = end(1, s) + big * (p + span * h)
            h = end(0, s) + big * h
        a, b = nothing, nothing
        for s in reversed(range(SEGS)):
            as_ref[group, s] = rl_rows * a
            b = end(3, s) + big * (b + span * a)
            a = end(2, s) + big * a
        res_sum = lam * res_x + res_near
        log_sum = lam * (log_x + res_x) + log_near
        rows = (h, p, a, b, res_sum, log_sum)
        for n, value in enumerate(rows):
            pay_ref[pl.ds(n * 8 + group, MODES, stride=SENT), :] = value
        return carry

    lax.fori_loop(0, groups, group_step, 0)


def chain_kernel(tokens, got_ref, rows_ref, skip_ref, back_ref):
    spans = got_ref.shape[0]
    groups = skip_ref.shape[0]
    own = lax.axis_index("ctx")

    def part(d, n):
        return got_ref[d, pl.ds(8 * n, 8), :]

    rate = jnp.concatenate(
        [rows_ref[3, group, pl.ds(own, 1), :] for group in range(groups)], axis=0
    )
    lam = jnp.exp(-rate)
    big = jnp.exp(rate * (-float(tokens)))
    span = float(tokens)
    zero = jnp.zeros((8, LANES), F32)
    h, p, res_x, log_x, res_sum, log_sum = (zero,) * 6
    for d in range(spans):
        back_ref[d, pl.ds(0, 8), :] = h
        a_d = part(d, 2)
        res_x = res_x + h * a_d
        log_x = log_x + (p * a_d + h * part(d, 3))
        res_sum = res_sum + part(d, 4)
        log_sum = log_sum + part(d, 5)
        p = part(d, 1) + big * (p + span * h)
        h = part(d, 0) + big * h
    a = zero
    for d in reversed(range(spans)):
        back_ref[d, pl.ds(8, 8), :] = a
        a = part(d, 2) + big * a
    res_total = res_sum + lam * res_x
    log_total = log_sum + lam * (log_x + res_x)
    for d in range(spans):
        back_ref[d, pl.ds(16, 8), :] = res_total
        back_ref[d, pl.ds(24, 8), :] = log_total
        back_ref[d, pl.ds(32, 8), :] = skip_ref[...]


def put(hbm, buf, sem, group):
    return pltpu.make_async_copy(buf.at[group], hbm.at[:, columns(group)], sem.at[group])


def natural_order(natural, seg_len):
    return jnp.concatenate([natural[pl.ds(s * PITCH, seg_len), :] for s in range(SEGS)], axis=0)


def entering(group, first, back_ref, rows_ref, local_ref, run, backward):
    big = rows_ref[0, group]
    state = rows_ref[1, group] * rows_of(back_ref, first + group, MODES, BACK)
    for s in reversed(range(SEGS)) if backward else range(SEGS):
        run[pl.ds(s, MODES, stride=SEGS), :] = local_ref[group, s] + state
        if s != (0 if backward else SEGS - 1):
            state = state * big


def far(total, indices, local_ref, group, k, lam_ref, mu_ref, run):
    for m in range(MODES):
        here = pl.ds(m * SEGS, SEGS)
        step = lam_ref[group, m]
        state = run[here, :]
        c = local_ref[group, k, m] + state
        run[here, :] = state * mu_ref[group, m]
        for i in indices:
            total[i] = total[i] + c
            if i != indices[-1]:
                c = c * step


def back_kernel(
    sq_ref, lam_ref, mu_ref, near_ref, rows_ref, al_ref, as_ref, back_ref,
    ig_ref,
    natural, run,
):
    groups, tokens, _ = ig_ref.shape
    seg_len = tokens // SEGS
    chunks = seg_len // SUB

    def group_step(group, carry):
        entering(group, 8, back_ref, rows_ref, as_ref, run, True)

        def chunk_step(step, carry):
            k = chunks - 1 - step
            near = [near_ref[group, d] for d in range(SUB)]
            ss = [sq_ref[group, k * SUB + j] for j in range(SUB)]
            total = []
            for j in range(SUB):
                value = near[0] * ss[j]
                for d in range(1, SUB - j):
                    value = value + near[d] * ss[j + d]
                total.append(value)
            far(total, list(reversed(range(SUB))), al_ref, group, k, lam_ref, mu_ref, run)
            for j in range(SUB):
                natural[pl.ds(k * SUB + j, SEGS, stride=PITCH), :] = total[j]
            return carry

        lax.fori_loop(0, chunks, chunk_step, 0, unroll=8)
        ig_ref[group] = natural_order(natural, seg_len).astype(jnp.bfloat16)
        return carry

    lax.fori_loop(0, groups, group_step, 0)


def gate_kernel(
    ig_buf, g_buf, xq_ref, lam_ref, mu_ref, near_ref, rows_ref, hl_ref, hs_ref, back_ref,
    ig_hbm, gg_hbm, late_ref,
    natural, run, buf, ig_sem, sem,
):
    groups, tokens, _ = g_buf.shape
    early = groups - LATE
    seg_len = tokens // SEGS
    chunks = seg_len // SUB
    for group in range(groups):
        put(ig_hbm, ig_buf, ig_sem, group).start()

    def group_step(group, carry):
        entering(group, 0, back_ref, rows_ref, hs_ref, run, False)

        def chunk_step(k, carry):
            near = [near_ref[group, d] for d in range(SUB)]
            xs = [xq_ref[group, k * SUB + j] for j in range(SUB)]
            total = []
            for i in range(SUB):
                value = near[0] * xs[i]
                for d in range(1, i + 1):
                    value = value + near[d] * xs[i - d]
                total.append(value)
            far(total, list(range(SUB)), hl_ref, group, k, lam_ref, mu_ref, run)
            for i in range(SUB):
                natural[pl.ds(k * SUB + i, SEGS, stride=PITCH), :] = total[i]
            return carry

        lax.fori_loop(0, chunks, chunk_step, 0, unroll=8)
        mixed = natural_order(natural, seg_len)
        gated = (g_buf[group].astype(F32) * mixed).astype(jnp.bfloat16)

        @pl.when(group < early)
        def _():
            buf[group] = gated
            put(gg_hbm, buf, sem, group).start()

        @pl.when(group >= early)
        def _():
            late_ref[group - early] = gated

        return carry

    lax.fori_loop(0, groups, group_step, 0)
    for group in range(groups):
        put(ig_hbm, ig_buf, ig_sem, group).wait()
        if group < early:
            put(gg_hbm, buf, sem, group).wait()


def totals(back_ref, rows_ref, group):
    res_raw = rows_of(back_ref, 16 + group, MODES, BACK)
    log_raw = rows_ref[2, group] * rows_of(back_ref, 24 + group, MODES, BACK)
    return res_raw, log_raw


def skip_total(back_ref):
    total = back_ref[pl.ds(32, 8), :]
    for span in range(1, back_ref.shape[0] // BACK):
        total = total + back_ref[pl.ds(span * BACK + 32, 8), :]
    return total


def norm_kernel(back_ref, rows_ref, sq_ref):
    groups = rows_ref.shape[1]
    res_sq = jnp.zeros((MODES, LANES), F32)
    log_sq = jnp.zeros((MODES, LANES), F32)
    for group in range(groups):
        res_raw, log_raw = totals(back_ref, rows_ref, group)
        res_sq = res_sq + res_raw * res_raw
        log_sq = log_sq + log_raw * log_raw
    skip = skip_total(back_ref)
    rows = [jnp.sum(v, axis=0, keepdims=True) for v in (res_sq, log_sq, skip * skip)]
    sq_ref[...] = jnp.concatenate(rows + [jnp.zeros((5, LANES), F32)], axis=0)


def scale_kernel(
    own_ref, other_ref, back_ref, rows_ref, late_ref, part_hbm,
    rg_hbm, lg_hbm, sg_hbm, gg_hbm,
    rg_buf, lg_buf, sg_buf, late_sem, sem,
):
    groups = rows_ref.shape[1]
    copies = [
        pltpu.make_async_copy(
            late_ref.at[n], gg_hbm.at[:, columns(groups - LATE + n)], late_sem.at[n]
        )
        for n in range(LATE)
    ]
    for copy in copies:
        copy.start()
    sums = jnp.sum(own_ref[...] + other_ref[...], axis=1, keepdims=True)

    def factor(n, ceiling):
        return jnp.minimum(1.0, ceiling / jnp.sqrt(sums[n : n + 1, :] + 1e-06))

    limit_modes = math.sqrt(MODES * CHANNELS)
    res_factor = factor(0, limit_modes)
    log_factor = factor(1, limit_modes)
    for group in range(groups):
        cols = pl.ds(group * LANES, LANES)
        res_raw, log_raw = totals(back_ref, rows_ref, group)
        rg_buf[:, cols] = res_raw * res_factor
        lg_buf[:, cols] = log_raw * log_factor
    sg_buf[...] = skip_total(back_ref) * factor(2, math.sqrt(CHANNELS))
    for n, (buf, hbm) in enumerate(((rg_buf, rg_hbm), (lg_buf, lg_hbm), (sg_buf, sg_hbm))):
        copy = pltpu.make_async_copy(buf, hbm, sem.at[n])
        copy.start()
        copies.append(copy)
    for copy in copies:
        copy.wait()


def params():
    return pltpu.CompilerParams(vmem_limit_bytes=VMEM_LIMIT)


def work(ops, moved):
    return pl.CostEstimate(flops=ops, bytes_accessed=moved, transcendentals=0)


HBM = pl.BlockSpec(memory_space=pltpu.HBM)
VMEM = pl.BlockSpec(memory_space=pltpu.VMEM)


def in_hbm(*arrays):
    return [pltpu.with_memory_space_constraint(array, pltpu.HBM) for array in arrays]


def shape(*dims):
    return jax.ShapeDtypeStruct(dims, F32)


def span_call(conv_input, out_gate, grad_out, pole_rate, residue, skip_gain):
    tokens, chan = conv_input.shape
    groups = chan // LANES
    seg_len = tokens // SEGS
    chunks = seg_len // SUB
    wide = pltpu.VMEM((AHEAD + 1, tokens, LANES), jnp.bfloat16)
    natural = pltpu.VMEM((SEGS * PITCH, LANES), F32)
    sems = pltpu.SemaphoreType.DMA((AHEAD + 1,))
    return pl.pallas_call(
        span_kernel,
        in_specs=[HBM] * 6,
        out_specs=[VMEM] * 13,
        out_shape=[
            shape(groups, chunks, MODES, SEGS, LANES),
            shape(groups, chunks, MODES, SEGS, LANES),
            shape(groups, SEGS, MODES, LANES),
            shape(groups, SEGS, MODES, LANES),
            shape(groups, seg_len, SEGS, LANES),
            shape(groups, seg_len, SEGS, LANES),
            shape(groups, MODES, SEGS, LANES),
            shape(groups, MODES, SEGS, LANES),
            shape(groups, SUB, SEGS, LANES),
            shape(4, groups, MODES, LANES),
            shape(groups, LANES),
            shape(MODES * SENT, LANES),
            jax.ShapeDtypeStruct((groups, tokens, LANES), jnp.bfloat16),
        ],
        scratch_shapes=[
            wide, wide,
            pltpu.VMEM((MODES, chan), F32),
            pltpu.VMEM((MODES, chan), F32),
            pltpu.VMEM((1, chan), F32),
            natural, natural,
            pltpu.VMEM((MODES, SEGS, LANES), F32),
            pltpu.VMEM((6, MODES * END_PITCH, LANES), F32),
            sems, sems, sems, pltpu.SemaphoreType.DMA((3,)),
        ],
        compiler_params=params(),
        name="span",
    )(
        *in_hbm(conv_input, out_gate, grad_out, pole_rate, residue, skip_gain.reshape(1, chan))
    )


def back_call(tokens, sq, lam, mu, near, rows, al, as_, back):
    groups = sq.shape[0]
    return pl.pallas_call(
        back_kernel,
        in_specs=[VMEM] * 8,
        out_specs=VMEM,
        out_shape=jax.ShapeDtypeStruct((groups, tokens, LANES), jnp.bfloat16),
        scratch_shapes=[
            pltpu.VMEM((SEGS * PITCH, LANES), F32),
            pltpu.VMEM((MODES * SEGS, LANES), F32),
        ],
        compiler_params=params(),
        cost_estimate=work(40 * MODES * tokens * groups * LANES, 16 * tokens * groups * LANES),
        name="adjoint",
    )(sq, lam, mu, near, rows, al, as_, back)


def gate_call(ig, g, xq, lam, mu, near, rows, hl, hs, back):
    groups, tokens, _ = g.shape
    chan = groups * LANES
    sems = pltpu.SemaphoreType.DMA((groups,))
    return pl.pallas_call(
        gate_kernel,
        in_specs=[VMEM] * 10,
        out_specs=[HBM, HBM, VMEM],
        out_shape=[
            jax.ShapeDtypeStruct((tokens, chan), jnp.bfloat16),
            jax.ShapeDtypeStruct((tokens, chan), jnp.bfloat16),
            jax.ShapeDtypeStruct((LATE, tokens, LANES), jnp.bfloat16),
        ],
        scratch_shapes=[
            pltpu.VMEM((SEGS * PITCH, LANES), F32),
            pltpu.VMEM((MODES * SEGS, LANES), F32),
            pltpu.VMEM((groups - LATE, tokens, LANES), jnp.bfloat16),
            sems, sems,
        ],
        compiler_params=params(),
        cost_estimate=work(40 * MODES * tokens * chan, 16 * tokens * chan),
        name="gate",
    )(ig, g, xq, lam, mu, near, rows, hl, hs, back)


def swapped(value, bit):
    peers = lax.axis_size("ch")
    return lax.ppermute(value, "ch", [(i, i ^ bit) for i in range(peers)])


def on_device(conv_input, out_gate, grad_out, pole_rate, residue, skip_gain):
    tokens, chan = conv_input.shape
    groups = chan // LANES
    spans = lax.axis_size("ctx")
    hl, al, hs, as_, xq, sq, lam, mu, near, rows, skip, pay, g = span_call(
        conv_input, out_gate, grad_out, pole_rate, residue, skip_gain
    )
    got = lax.all_to_all(pay.reshape(spans, SENT, LANES), "ctx", 0, 0)
    back = pl.pallas_call(
        functools.partial(chain_kernel, tokens),
        out_shape=shape(spans, BACK, LANES),
        compiler_params=params(),
        name="chain",
    )(got, rows, skip)
    back = lax.all_to_all(back, "ctx", 0, 0).reshape(MODES * BACK, LANES)

    squares = pl.pallas_call(
        norm_kernel,
        out_shape=shape(8, LANES),
        compiler_params=params(),
        name="norm",
    )(back, rows)
    first = swapped(squares, 2)
    ig = back_call(tokens, sq, lam, mu, near, rows, al, as_, back)
    first, ig = lax.optimization_barrier((first, ig))
    squares = squares + first
    second = swapped(squares, 4)
    input_grad, gate_grad, late = gate_call(ig, g, xq, lam, mu, near, rows, hl, hs, back)
    second, late = lax.optimization_barrier((second, late))
    squares = squares + second
    other = swapped(squares, 1)
    res_out, log_out, skip_out, gate_grad = pl.pallas_call(
        scale_kernel,
        in_specs=[VMEM] * 5 + [HBM],
        out_specs=[HBM] * 4,
        out_shape=[
            shape(MODES, chan), shape(MODES, chan), shape(groups, LANES),
            jax.ShapeDtypeStruct((tokens, chan), jnp.bfloat16),
        ],
        scratch_shapes=[
            pltpu.VMEM((MODES, chan), F32),
            pltpu.VMEM((MODES, chan), F32),
            pltpu.VMEM((groups, LANES), F32),
            pltpu.SemaphoreType.DMA((LATE,)),
            pltpu.SemaphoreType.DMA((3,)),
        ],
        input_output_aliases={5: 3},
        compiler_params=params(),
        name="scale",
    )(squares, other, back, rows, late, gate_grad)
    return input_grad, gate_grad, res_out, log_out, skip_out.reshape(chan)


def solution(mesh):
    in_specs = (
        P("ctx", "ch"), P("ctx", "ch"), P("ctx", "ch"), P(None, "ch"), P(None, "ch"), P("ch"),
    )
    out_specs = (P("ctx", "ch"), P("ctx", "ch"), P(None, "ch"), P(None, "ch"), P("ch"))
    return jax.shard_map(
        on_device, mesh=mesh, in_specs=in_specs, out_specs=out_specs, check_vma=False
    )
```

```python
import functools
import math

import jax
import jax.numpy as jnp
from jax import lax
from jax.experimental import pallas as pl
from jax.experimental.pallas import tpu as pltpu
from jax.sharding import PartitionSpec as P

CHANNELS = 8192
MODES = 16
LANES = 128
SEGS = 8
SUB = 8
F32 = jnp.float32
LATE = 2
AHEAD = 2
END_PITCH = 9
SENT = 48
BACK = 40
PITCH = 72
VMEM_LIMIT = 16 * 1024 * 1024


def rows_of(ref, start, count, stride):
    return ref[pl.ds(start, count, stride=stride), :]


def spread(values):
    return jnp.broadcast_to(values, (SEGS, LANES))


def columns(group):
    return pl.ds(pl.multiple_of(group * LANES, LANES), LANES)


def span_kernel(
    x_hbm, o_hbm, g_hbm, rate_hbm, res_hbm, gain_hbm,
    hl_ref, al_ref, hs_ref, as_ref, xq_ref, sq_ref, lam_ref, mu_ref, near_ref, rows_ref, skip_ref, pay_ref, g_buf,
    x_buf, o_buf, rate_buf, res_buf, gain_buf,
    natural, second, rl_t, ends,
    x_sem, o_sem, g_sem, small_sem,
):
    tokens = x_buf.shape[1]
    groups = xq_ref.shape[0]
    seg_len = tokens // SEGS
    chunks = seg_len // SUB
    small = [
        pltpu.make_async_copy(hbm, buf, small_sem.at[n])
        for n, (hbm, buf) in enumerate(
            ((rate_hbm, rate_buf), (res_hbm, res_buf), (gain_hbm, gain_buf))
        )
    ]

    def blocks(group, slot):
        return [
            pltpu.make_async_copy(hbm.at[:, columns(group)], buf, sem.at[slot])
            for hbm, buf, sem in (
                (x_hbm, x_buf.at[slot], x_sem),
                (o_hbm, o_buf.at[slot], o_sem),
                (g_hbm, g_buf.at[group], g_sem),
            )
        ]

    for copy in blocks(0, 0) + small:
        copy.start()
    for group in range(1, min(AHEAD, groups)):
        for copy in blocks(group, group):
            copy.start()
    for copy in small:
        copy.wait()
    zero = jnp.zeros((SEGS, LANES), F32)

    def group_step(group, carry):
        slot = lax.rem(group, AHEAD + 1)

        @pl.when(group + AHEAD < groups)
        def _():
            for copy in blocks(group + AHEAD, lax.rem(group + AHEAD, AHEAD + 1)):
                copy.start()

        cols = columns(group)
        rate = rate_buf[:, cols]
        residue = res_buf[:, cols]
        lam = jnp.exp(-rate)
        mu_rows = jnp.exp(rate * (-float(SUB)))
        big = jnp.exp(rate * (-float(seg_len)))
        rl_rows = residue * lam
        for m in range(MODES):
            lam_ref[group, m] = spread(lam[m : m + 1, :])
            mu_ref[group, m] = spread(mu_rows[m : m + 1, :])
            rl_t[m] = spread(rl_rows[m : m + 1, :])
        rows_ref[0, group] = big
        rows_ref[1, group] = rl_rows
        rows_ref[2, group] = -(rate * residue)
        rows_ref[3, group] = rate
        term = residue
        for d in range(SUB):
            row = jnp.sum(term, axis=0, keepdims=True)
            if d == 0:
                row = row + gain_buf[:, cols]
            near_ref[group, d] = spread(row)
            term = term * lam

        xq = xq_ref.at[group]
        sq = sq_ref.at[group]
        for copy in blocks(group, slot):
            copy.wait()
        for s in range(SEGS):
            part = pl.ds(s * seg_len, seg_len)
            source = x_buf[slot, part, :].astype(F32)
            signal = g_buf[group, part, :].astype(F32) * o_buf[slot, part, :].astype(F32)
            natural[pl.ds(s * PITCH, seg_len), :] = source
            second[pl.ds(s * PITCH, seg_len), :] = signal

        def lag_step(k, acc):
            xs = [rows_of(natural, k * SUB + j, SEGS, PITCH) for j in range(SUB)]
            ss = [rows_of(second, k * SUB + j, SEGS, PITCH) for j in range(SUB)]
            for j in range(SUB):
                xq[k * SUB + j] = xs[j]
                sq[k * SUB + j] = ss[j]
            out = []
            for d in range(SUB):
                total = acc[d]
                for i in range(d, SUB):
                    total = total + ss[i] * xs[i - d]
                out.append(total)
            return tuple(out)

        lagged = lax.fori_loop(0, chunks, lag_step, (zero,) * SUB, unroll=8)
        lag_rows = [jnp.sum(v, axis=0, keepdims=True) for v in lagged]
        skip_ref[pl.ds(group, 1), :] = lag_rows[0]
        res_near = jnp.broadcast_to(lag_rows[0], lam.shape)
        log_near = jnp.zeros_like(lam)
        power = lam
        for d in range(1, SUB):
            term = power * lag_rows[d]
            res_near = res_near + term
            log_near = log_near + float(d) * term
            power = power * lam

        def mode_step(m, carry):
            p1 = lam_ref[group, m]
            mu = mu_ref[group, m]
            rl = rl_t[m]
            p2 = p1 * p1
            p3 = p2 * p1
            p4 = p2 * p2
            pw = [None, p1, p2, p3, p4, p4 * p1, p3 * p3, p4 * p3]
            a_parts = [None] * chunks
            b_parts = [None] * chunks
            for k in reversed(range(chunks)):
                a = sq[k * SUB + SUB - 1] * pw[SUB - 1]
                b = a
                for i in reversed(range(1, SUB - 1)):
                    a = a + sq[k * SUB + i] * pw[i]
                    b = b + a
                a = a + sq[k * SUB]
                a_parts[k] = a
                b_parts[k] = b
                if k == chunks - 1:
                    al_ref[group, k, m] = zero
                    a_run = a
                    b_run = b
                else:
                    al_ref[group, k, m] = rl * a_run
                    b_run = b + mu * (b_run + float(SUB) * a_run)
                    a_run = a + mu * a_run
            for k in range(chunks):
                h = xq[k * SUB] * pw[SUB - 1]
                p = h
                for j in range(1, SUB - 1):
                    h = h + xq[k * SUB + j] * pw[SUB - 1 - j]
                    p = p + h
                h = h + xq[k * SUB + SUB - 1]
                if k == 0:
                    hl_ref[group, k, m] = zero
                    h_run = h
                    p_run = p
                    continue
                hl_ref[group, k, m] = rl * h_run
                res_new = h_run * a_parts[k]
                log_new = p_run * a_parts[k] + h_run * b_parts[k]
                res_x = res_new if k == 1 else res_x + res_new
                log_x = log_new if k == 1 else log_x + log_new
                p_run = p + mu * (p_run + float(SUB) * h_run)
                h_run = h + mu * h_run
            for n, value in enumerate((h_run, p_run, a_run, b_run, res_x, log_x)):
                ends[n, pl.ds(m * END_PITCH, SEGS), :] = value
            return carry

        lax.fori_loop(0, MODES, mode_step, 0, unroll=16)

        def end(n, s):
            return ends[n, pl.ds(s, MODES, stride=END_PITCH), :]

        span = float(seg_len)
        nothing = jnp.zeros_like(lam)
        h, p, res_x, log_x = nothing, nothing, nothing, nothing
        for s in range(SEGS):
            hs_ref[group, s] = rl_rows * h
            a_s, b_s = end(2, s), end(3, s)
            res_x = res_x + end(4, s) + h * a_s
            log_x = log_x + end(5, s) + (p * a_s + h * b_s)
            p = end(1, s) + big * (p + span * h)
            h = end(0, s) + big * h
        a, b = nothing, nothing
        for s in reversed(range(SEGS)):
            as_ref[group, s] = rl_rows * a
            b = end(3, s) + big * (b + span * a)
            a = end(2, s) + big * a
        res_sum = lam * res_x + res_near
        log_sum = lam * (log_x + res_x) + log_near
        rows = (h, p, a, b, res_sum, log_sum)
        for n, value in enumerate(rows):
            pay_ref[pl.ds(n * 8 + group, MODES, stride=SENT), :] = value
        return carry

    lax.fori_loop(0, groups, group_step, 0)


def chain_kernel(tokens, got_ref, rows_ref, skip_ref, back_ref):
    spans = got_ref.shape[0]
    groups = skip_ref.shape[0]
    own = lax.axis_index("ctx")

    def part(d, n):
        return got_ref[d, pl.ds(8 * n, 8), :]

    rate = jnp.concatenate(
        [rows_ref[3, group, pl.ds(own, 1), :] for group in range(groups)], axis=0
    )
    lam = jnp.exp(-rate)
    big = jnp.exp(rate * (-float(tokens)))
    span = float(tokens)
    zero = jnp.zeros((8, LANES), F32)
    h, p, res_x, log_x, res_sum, log_sum = (zero,) * 6
    for d in range(spans):
        back_ref[d, pl.ds(0, 8), :] = h
        a_d = part(d, 2)
        res_x = res_x + h * a_d
        log_x = log_x + (p * a_d + h * part(d, 3))
        res_sum = res_sum + part(d, 4)
        log_sum = log_sum + part(d, 5)
        p = part(d, 1) + big * (p + span * h)
        h = part(d, 0) + big * h
    a = zero
    for d in reversed(range(spans)):
        back_ref[d, pl.ds(8, 8), :] = a
        a = part(d, 2) + big * a
    res_total = res_sum + lam * res_x
    log_total = log_sum + lam * (log_x + res_x)
    for d in range(spans):
        back_ref[d, pl.ds(16, 8), :] = res_total
        back_ref[d, pl.ds(24, 8), :] = log_total
        back_ref[d, pl.ds(32, 8), :] = skip_ref[...]


def put(hbm, buf, sem, group):
    return pltpu.make_async_copy(buf.at[group], hbm.at[:, columns(group)], sem.at[group])


def natural_order(natural, seg_len):
    return jnp.concatenate([natural[pl.ds(s * PITCH, seg_len), :] for s in range(SEGS)], axis=0)


def entering(group, first, back_ref, rows_ref, local_ref, run, backward):
    big = rows_ref[0, group]
    state = rows_ref[1, group] * rows_of(back_ref, first + group, MODES, BACK)
    for s in reversed(range(SEGS)) if backward else range(SEGS):
        run[pl.ds(s, MODES, stride=SEGS), :] = local_ref[group, s] + state
        if s != (0 if backward else SEGS - 1):
            state = state * big


def far(total, indices, local_ref, group, k, lam_ref, mu_ref, run):
    for m in range(MODES):
        here = pl.ds(m * SEGS, SEGS)
        step = lam_ref[group, m]
        state = run[here, :]
        c = local_ref[group, k, m] + state
        run[here, :] = state * mu_ref[group, m]
        for i in indices:
            total[i] = total[i] + c
            if i != indices[-1]:
                c = c * step


def back_kernel(
    sq_ref, lam_ref, mu_ref, near_ref, rows_ref, al_ref, as_ref, back_ref,
    ig_ref,
    natural, run,
):
    groups, tokens, _ = ig_ref.shape
    seg_len = tokens // SEGS
    chunks = seg_len // SUB

    def group_step(group, carry):
        entering(group, 8, back_ref, rows_ref, as_ref, run, True)

        def chunk_step(step, carry):
            k = chunks - 1 - step
            near = [near_ref[group, d] for d in range(SUB)]
            ss = [sq_ref[group, k * SUB + j] for j in range(SUB)]
            total = []
            for j in range(SUB):
                value = near[0] * ss[j]
                for d in range(1, SUB - j):
                    value = value + near[d] * ss[j + d]
                total.append(value)
            far(total, list(reversed(range(SUB))), al_ref, group, k, lam_ref, mu_ref, run)
            for j in range(SUB):
                natural[pl.ds(k * SUB + j, SEGS, stride=PITCH), :] = total[j]
            return carry

        lax.fori_loop(0, chunks, chunk_step, 0, unroll=8)
        ig_ref[group] = natural_order(natural, seg_len).astype(jnp.bfloat16)
        return carry

    lax.fori_loop(0, groups, group_step, 0)


def gate_kernel(
    ig_buf, g_buf, xq_ref, lam_ref, mu_ref, near_ref, rows_ref, hl_ref, hs_ref, back_ref,
    ig_hbm, gg_hbm, late_ref,
    natural, run, buf, ig_sem, sem,
):
    groups, tokens, _ = g_buf.shape
    early = groups - LATE
    seg_len = tokens // SEGS
    chunks = seg_len // SUB
    for group in range(groups):
        put(ig_hbm, ig_buf, ig_sem, group).start()

    def group_step(group, carry):
        entering(group, 0, back_ref, rows_ref, hs_ref, run, False)

        def chunk_step(k, carry):
            near = [near_ref[group, d] for d in range(SUB)]
            xs = [xq_ref[group, k * SUB + j] for j in range(SUB)]
            total = []
            for i in range(SUB):
                value = near[0] * xs[i]
                for d in range(1, i + 1):
                    value = value + near[d] * xs[i - d]
                total.append(value)
            far(total, list(range(SUB)), hl_ref, group, k, lam_ref, mu_ref, run)
            for i in range(SUB):
                natural[pl.ds(k * SUB + i, SEGS, stride=PITCH), :] = total[i]
            return carry

        lax.fori_loop(0, chunks, chunk_step, 0, unroll=8)
        mixed = natural_order(natural, seg_len)
        gated = (g_buf[group].astype(F32) * mixed).astype(jnp.bfloat16)

        @pl.when(group < early)
        def _():
            buf[group] = gated
            put(gg_hbm, buf, sem, group).start()

        @pl.when(group >= early)
        def _():
            late_ref[group - early] = gated

        return carry

    lax.fori_loop(0, groups, group_step, 0)
    for group in range(groups):
        put(ig_hbm, ig_buf, ig_sem, group).wait()
        if group < early:
            put(gg_hbm, buf, sem, group).wait()


def totals(back_ref, rows_ref, group):
    res_raw = rows_of(back_ref, 16 + group, MODES, BACK)
    log_raw = rows_ref[2, group] * rows_of(back_ref, 24 + group, MODES, BACK)
    return res_raw, log_raw


def skip_total(back_ref):
    total = back_ref[pl.ds(32, 8), :]
    for span in range(1, back_ref.shape[0] // BACK):
        total = total + back_ref[pl.ds(span * BACK + 32, 8), :]
    return total


def norm_kernel(back_ref, rows_ref, sq_ref):
    groups = rows_ref.shape[1]
    res_sq = jnp.zeros((MODES, LANES), F32)
    log_sq = jnp.zeros((MODES, LANES), F32)
    for group in range(groups):
        res_raw, log_raw = totals(back_ref, rows_ref, group)
        res_sq = res_sq + res_raw * res_raw
        log_sq = log_sq + log_raw * log_raw
    skip = skip_total(back_ref)
    rows = [jnp.sum(v, axis=0, keepdims=True) for v in (res_sq, log_sq, skip * skip)]
    sq_ref[...] = jnp.concatenate(rows + [jnp.zeros((5, LANES), F32)], axis=0)


def scale_kernel(
    own_ref, first_ref, second_ref, third_ref, back_ref, rows_ref, late_ref, part_hbm,
    rg_hbm, lg_hbm, sg_hbm, gg_hbm,
    rg_buf, lg_buf, sg_buf, late_sem, sem,
):
    groups = rows_ref.shape[1]
    copies = [
        pltpu.make_async_copy(
            late_ref.at[n], gg_hbm.at[:, columns(groups - LATE + n)], late_sem.at[n]
        )
        for n in range(LATE)
    ]
    for copy in copies:
        copy.start()
    total = (own_ref[...] + first_ref[...]) + (second_ref[...] + third_ref[...])
    sums = jnp.sum(total, axis=1, keepdims=True)

    def factor(n, ceiling):
        return jnp.minimum(1.0, ceiling / jnp.sqrt(sums[n : n + 1, :] + 1e-06))

    limit_modes = math.sqrt(MODES * CHANNELS)
    res_factor = factor(0, limit_modes)
    log_factor = factor(1, limit_modes)
    for group in range(groups):
        cols = pl.ds(group * LANES, LANES)
        res_raw, log_raw = totals(back_ref, rows_ref, group)
        rg_buf[:, cols] = res_raw * res_factor
        lg_buf[:, cols] = log_raw * log_factor
    sg_buf[...] = skip_total(back_ref) * factor(2, math.sqrt(CHANNELS))
    for n, (buf, hbm) in enumerate(((rg_buf, rg_hbm), (lg_buf, lg_hbm), (sg_buf, sg_hbm))):
        copy = pltpu.make_async_copy(buf, hbm, sem.at[n])
        copy.start()
        copies.append(copy)
    for copy in copies:
        copy.wait()


def params():
    return pltpu.CompilerParams(vmem_limit_bytes=VMEM_LIMIT)


def work(ops, moved):
    return pl.CostEstimate(flops=ops, bytes_accessed=moved, transcendentals=0)


HBM = pl.BlockSpec(memory_space=pltpu.HBM)
VMEM = pl.BlockSpec(memory_space=pltpu.VMEM)


def in_hbm(*arrays):
    return [pltpu.with_memory_space_constraint(array, pltpu.HBM) for array in arrays]


def shape(*dims):
    return jax.ShapeDtypeStruct(dims, F32)


def span_call(conv_input, out_gate, grad_out, pole_rate, residue, skip_gain):
    tokens, chan = conv_input.shape
    groups = chan // LANES
    seg_len = tokens // SEGS
    chunks = seg_len // SUB
    wide = pltpu.VMEM((AHEAD + 1, tokens, LANES), jnp.bfloat16)
    natural = pltpu.VMEM((SEGS * PITCH, LANES), F32)
    sems = pltpu.SemaphoreType.DMA((AHEAD + 1,))
    return pl.pallas_call(
        span_kernel,
        in_specs=[HBM] * 6,
        out_specs=[VMEM] * 13,
        out_shape=[
            shape(groups, chunks, MODES, SEGS, LANES),
            shape(groups, chunks, MODES, SEGS, LANES),
            shape(groups, SEGS, MODES, LANES),
            shape(groups, SEGS, MODES, LANES),
            shape(groups, seg_len, SEGS, LANES),
            shape(groups, seg_len, SEGS, LANES),
            shape(groups, MODES, SEGS, LANES),
            shape(groups, MODES, SEGS, LANES),
            shape(groups, SUB, SEGS, LANES),
            shape(4, groups, MODES, LANES),
            shape(groups, LANES),
            shape(MODES * SENT, LANES),
            jax.ShapeDtypeStruct((groups, tokens, LANES), jnp.bfloat16),
        ],
        scratch_shapes=[
            wide, wide,
            pltpu.VMEM((MODES, chan), F32),
            pltpu.VMEM((MODES, chan), F32),
            pltpu.VMEM((1, chan), F32),
            natural, natural,
            pltpu.VMEM((MODES, SEGS, LANES), F32),
            pltpu.VMEM((6, MODES * END_PITCH, LANES), F32),
            sems, sems, sems, pltpu.SemaphoreType.DMA((3,)),
        ],
        compiler_params=params(),
        name="span",
    )(
        *in_hbm(conv_input, out_gate, grad_out, pole_rate, residue, skip_gain.reshape(1, chan))
    )


def back_call(tokens, sq, lam, mu, near, rows, al, as_, back):
    groups = sq.shape[0]
    return pl.pallas_call(
        back_kernel,
        in_specs=[VMEM] * 8,
        out_specs=VMEM,
        out_shape=jax.ShapeDtypeStruct((groups, tokens, LANES), jnp.bfloat16),
        scratch_shapes=[
            pltpu.VMEM((SEGS * PITCH, LANES), F32),
            pltpu.VMEM((MODES * SEGS, LANES), F32),
        ],
        compiler_params=params(),
        cost_estimate=work(40 * MODES * tokens * groups * LANES, 16 * tokens * groups * LANES),
        name="adjoint",
    )(sq, lam, mu, near, rows, al, as_, back)


def gate_call(ig, g, xq, lam, mu, near, rows, hl, hs, back):
    groups, tokens, _ = g.shape
    chan = groups * LANES
    sems = pltpu.SemaphoreType.DMA((groups,))
    return pl.pallas_call(
        gate_kernel,
        in_specs=[VMEM] * 10,
        out_specs=[HBM, HBM, VMEM],
        out_shape=[
            jax.ShapeDtypeStruct((tokens, chan), jnp.bfloat16),
            jax.ShapeDtypeStruct((tokens, chan), jnp.bfloat16),
            jax.ShapeDtypeStruct((LATE, tokens, LANES), jnp.bfloat16),
        ],
        scratch_shapes=[
            pltpu.VMEM((SEGS * PITCH, LANES), F32),
            pltpu.VMEM((MODES * SEGS, LANES), F32),
            pltpu.VMEM((groups - LATE, tokens, LANES), jnp.bfloat16),
            sems, sems,
        ],
        compiler_params=params(),
        cost_estimate=work(40 * MODES * tokens * chan, 16 * tokens * chan),
        name="gate",
    )(ig, g, xq, lam, mu, near, rows, hl, hs, back)


def swapped(value, bit):
    peers = lax.axis_size("ch")
    return lax.ppermute(value, "ch", [(i, i ^ bit) for i in range(peers)])


def on_device(conv_input, out_gate, grad_out, pole_rate, residue, skip_gain):
    tokens, chan = conv_input.shape
    groups = chan // LANES
    spans = lax.axis_size("ctx")
    hl, al, hs, as_, xq, sq, lam, mu, near, rows, skip, pay, g = span_call(
        conv_input, out_gate, grad_out, pole_rate, residue, skip_gain
    )
    got = lax.all_to_all(pay.reshape(spans, SENT, LANES), "ctx", 0, 0)
    back = pl.pallas_call(
        functools.partial(chain_kernel, tokens),
        out_shape=shape(spans, BACK, LANES),
        compiler_params=params(),
        name="chain",
    )(got, rows, skip)
    back = lax.all_to_all(back, "ctx", 0, 0).reshape(MODES * BACK, LANES)

    squares = pl.pallas_call(
        norm_kernel,
        out_shape=shape(8, LANES),
        compiler_params=params(),
        name="norm",
    )(back, rows)
    squares = squares + swapped(squares, 1)
    others = [swapped(squares, bit) for bit in (2, 4, 6)]
    ig = back_call(tokens, sq, lam, mu, near, rows, al, as_, back)
    input_grad, gate_grad, late = gate_call(ig, g, xq, lam, mu, near, rows, hl, hs, back)
    *others, late = lax.optimization_barrier((*others, late))
    res_out, log_out, skip_out, gate_grad = pl.pallas_call(
        scale_kernel,
        in_specs=[VMEM] * 7 + [HBM],
        out_specs=[HBM] * 4,
        out_shape=[
            shape(MODES, chan), shape(MODES, chan), shape(groups, LANES),
            jax.ShapeDtypeStruct((tokens, chan), jnp.bfloat16),
        ],
        scratch_shapes=[
            pltpu.VMEM((MODES, chan), F32),
            pltpu.VMEM((MODES, chan), F32),
            pltpu.VMEM((groups, LANES), F32),
            pltpu.SemaphoreType.DMA((LATE,)),
            pltpu.SemaphoreType.DMA((3,)),
        ],
        input_output_aliases={7: 3},
        compiler_params=params(),
        name="scale",
    )(squares, *others, back, rows, late, gate_grad)
    return input_grad, gate_grad, res_out, log_out, skip_out.reshape(chan)


def solution(mesh):
    in_specs = (
        P("ctx", "ch"), P("ctx", "ch"), P("ctx", "ch"), P(None, "ch"), P(None, "ch"), P("ch"),
    )
    out_specs = (P("ctx", "ch"), P("ctx", "ch"), P(None, "ch"), P(None, "ch"), P("ch"))
    return jax.shard_map(
        on_device, mesh=mesh, in_specs=in_specs, out_specs=out_specs, check_vma=False
    )
```

```python
import functools
import math

import jax
import jax.numpy as jnp
from jax import lax
from jax.experimental import pallas as pl
from jax.experimental.pallas import tpu as pltpu
from jax.sharding import PartitionSpec as P

CHANNELS = 8192
MODES = 16
LANES = 128
SEGS = 8
SUB = 8
F32 = jnp.float32
FIRST = 6
LATE = 2
AHEAD = 2
END_PITCH = 9
SENT = 48
BACK = 40
PITCH = 72
VMEM_LIMIT = 16 * 1024 * 1024


def rows_of(ref, start, count, stride):
    return ref[pl.ds(start, count, stride=stride), :]


def spread(values):
    return jnp.broadcast_to(values, (SEGS, LANES))


def columns(group):
    return pl.ds(pl.multiple_of(group * LANES, LANES), LANES)


def span_kernel(
    x_hbm, o_hbm, g_hbm, rate_hbm, res_hbm, gain_hbm,
    hl_ref, al_ref, hs_ref, as_ref, xq_ref, sq_ref, lam_ref, mu_ref, near_ref, rows_ref, skip_ref, pay_ref, g_buf,
    x_buf, o_buf, rate_buf, res_buf, gain_buf,
    natural, second, rl_t, ends,
    x_sem, o_sem, g_sem, small_sem,
):
    tokens = x_buf.shape[1]
    groups = xq_ref.shape[0]
    seg_len = tokens // SEGS
    chunks = seg_len // SUB
    small = [
        pltpu.make_async_copy(hbm, buf, small_sem.at[n])
        for n, (hbm, buf) in enumerate(
            ((rate_hbm, rate_buf), (res_hbm, res_buf), (gain_hbm, gain_buf))
        )
    ]

    def blocks(group, slot):
        return [
            pltpu.make_async_copy(hbm.at[:, columns(group)], buf, sem.at[slot])
            for hbm, buf, sem in (
                (x_hbm, x_buf.at[slot], x_sem),
                (o_hbm, o_buf.at[slot], o_sem),
                (g_hbm, g_buf.at[group], g_sem),
            )
        ]

    for copy in blocks(0, 0) + small:
        copy.start()
    for group in range(1, min(AHEAD, groups)):
        for copy in blocks(group, group):
            copy.start()
    for copy in small:
        copy.wait()
    zero = jnp.zeros((SEGS, LANES), F32)

    def group_step(group, carry):
        slot = lax.rem(group, AHEAD + 1)

        @pl.when(group + AHEAD < groups)
        def _():
            for copy in blocks(group + AHEAD, lax.rem(group + AHEAD, AHEAD + 1)):
                copy.start()

        cols = columns(group)
        rate = rate_buf[:, cols]
        residue = res_buf[:, cols]
        lam = jnp.exp(-rate)
        mu_rows = jnp.exp(rate * (-float(SUB)))
        big = jnp.exp(rate * (-float(seg_len)))
        rl_rows = residue * lam
        for m in range(MODES):
            lam_ref[group, m] = spread(lam[m : m + 1, :])
            mu_ref[group, m] = spread(mu_rows[m : m + 1, :])
            rl_t[m] = spread(rl_rows[m : m + 1, :])
        rows_ref[0, group] = big
        rows_ref[1, group] = rl_rows
        rows_ref[2, group] = -(rate * residue)
        rows_ref[3, group] = rate
        term = residue
        for d in range(SUB):
            row = jnp.sum(term, axis=0, keepdims=True)
            if d == 0:
                row = row + gain_buf[:, cols]
            near_ref[group, d] = spread(row)
            term = term * lam

        xq = xq_ref.at[group]
        sq = sq_ref.at[group]
        for copy in blocks(group, slot):
            copy.wait()
        for s in range(SEGS):
            part = pl.ds(s * seg_len, seg_len)
            source = x_buf[slot, part, :].astype(F32)
            signal = g_buf[group, part, :].astype(F32) * o_buf[slot, part, :].astype(F32)
            natural[pl.ds(s * PITCH, seg_len), :] = source
            second[pl.ds(s * PITCH, seg_len), :] = signal

        def lag_step(k, acc):
            xs = [rows_of(natural, k * SUB + j, SEGS, PITCH) for j in range(SUB)]
            ss = [rows_of(second, k * SUB + j, SEGS, PITCH) for j in range(SUB)]
            for j in range(SUB):
                xq[k * SUB + j] = xs[j]
                sq[k * SUB + j] = ss[j]
            out = []
            for d in range(SUB):
                total = acc[d]
                for i in range(d, SUB):
                    total = total + ss[i] * xs[i - d]
                out.append(total)
            return tuple(out)

        lagged = lax.fori_loop(0, chunks, lag_step, (zero,) * SUB, unroll=8)
        lag_rows = [jnp.sum(v, axis=0, keepdims=True) for v in lagged]
        skip_ref[pl.ds(group, 1), :] = lag_rows[0]
        res_near = jnp.broadcast_to(lag_rows[0], lam.shape)
        log_near = jnp.zeros_like(lam)
        power = lam
        for d in range(1, SUB):
            term = power * lag_rows[d]
            res_near = res_near + term
            log_near = log_near + float(d) * term
            power = power * lam

        def mode_step(m, carry):
            p1 = lam_ref[group, m]
            mu = mu_ref[group, m]
            rl = rl_t[m]
            p2 = p1 * p1
            p3 = p2 * p1
            p4 = p2 * p2
            pw = [None, p1, p2, p3, p4, p4 * p1, p3 * p3, p4 * p3]
            a_parts = [None] * chunks
            b_parts = [None] * chunks
            for k in reversed(range(chunks)):
                a = sq[k * SUB + SUB - 1] * pw[SUB - 1]
                b = a
                for i in reversed(range(1, SUB - 1)):
                    a = a + sq[k * SUB + i] * pw[i]
                    b = b + a
                a = a + sq[k * SUB]
                a_parts[k] = a
                b_parts[k] = b
                if k == chunks - 1:
                    al_ref[group, k, m] = zero
                    a_run = a
                    b_run = b
                else:
                    al_ref[group, k, m] = rl * a_run
                    b_run = b + mu * (b_run + float(SUB) * a_run)
                    a_run = a + mu * a_run
            for k in range(chunks):
                h = xq[k * SUB] * pw[SUB - 1]
                p = h
                for j in range(1, SUB - 1):
                    h = h + xq[k * SUB + j] * pw[SUB - 1 - j]
                    p = p + h
                h = h + xq[k * SUB + SUB - 1]
                if k == 0:
                    hl_ref[group, k, m] = zero
                    h_run = h
                    p_run = p
                    continue
                hl_ref[group, k, m] = rl * h_run
                res_new = h_run * a_parts[k]
                log_new = p_run * a_parts[k] + h_run * b_parts[k]
                res_x = res_new if k == 1 else res_x + res_new
                log_x = log_new if k == 1 else log_x + log_new
                p_run = p + mu * (p_run + float(SUB) * h_run)
                h_run = h + mu * h_run
            for n, value in enumerate((h_run, p_run, a_run, b_run, res_x, log_x)):
                ends[n, pl.ds(m * END_PITCH, SEGS), :] = value
            return carry

        lax.fori_loop(0, MODES, mode_step, 0, unroll=16)

        def end(n, s):
            return ends[n, pl.ds(s, MODES, stride=END_PITCH), :]

        span = float(seg_len)
        nothing = jnp.zeros_like(lam)
        h, p, res_x, log_x = nothing, nothing, nothing, nothing
        for s in range(SEGS):
            hs_ref[group, s] = rl_rows * h
            a_s, b_s = end(2, s), end(3, s)
            res_x = res_x + end(4, s) + h * a_s
            log_x = log_x + end(5, s) + (p * a_s + h * b_s)
            p = end(1, s) + big * (p + span * h)
            h = end(0, s) + big * h
        a, b = nothing, nothing
        for s in reversed(range(SEGS)):
            as_ref[group, s] = rl_rows * a
            b = end(3, s) + big * (b + span * a)
            a = end(2, s) + big * a
        res_sum = lam * res_x + res_near
        log_sum = lam * (log_x + res_x) + log_near
        rows = (h, p, a, b, res_sum, log_sum)
        for n, value in enumerate(rows):
            pay_ref[pl.ds(n * 8 + group, MODES, stride=SENT), :] = value
        return carry

    lax.fori_loop(0, groups, group_step, 0)


def chain_kernel(tokens, got_ref, rows_ref, skip_ref, back_ref):
    spans = got_ref.shape[0]
    groups = skip_ref.shape[0]
    own = lax.axis_index("ctx")

    def part(d, n):
        return got_ref[d, pl.ds(8 * n, 8), :]

    rate = jnp.concatenate(
        [rows_ref[3, group, pl.ds(own, 1), :] for group in range(groups)], axis=0
    )
    lam = jnp.exp(-rate)
    big = jnp.exp(rate * (-float(tokens)))
    span = float(tokens)
    zero = jnp.zeros((8, LANES), F32)
    h, p, res_x, log_x, res_sum, log_sum = (zero,) * 6
    for d in range(spans):
        back_ref[d, pl.ds(0, 8), :] = h
        a_d = part(d, 2)
        res_x = res_x + h * a_d
        log_x = log_x + (p * a_d + h * part(d, 3))
        res_sum = res_sum + part(d, 4)
        log_sum = log_sum + part(d, 5)
        p = part(d, 1) + big * (p + span * h)
        h = part(d, 0) + big * h
    a = zero
    for d in reversed(range(spans)):
        back_ref[d, pl.ds(8, 8), :] = a
        a = part(d, 2) + big * a
    res_total = res_sum + lam * res_x
    log_total = log_sum + lam * (log_x + res_x)
    for d in range(spans):
        back_ref[d, pl.ds(16, 8), :] = res_total
        back_ref[d, pl.ds(24, 8), :] = log_total
        back_ref[d, pl.ds(32, 8), :] = skip_ref[...]


def put(hbm, buf, sem, group):
    return pltpu.make_async_copy(buf.at[group], hbm.at[:, columns(group)], sem.at[group])


def natural_order(natural, seg_len):
    return jnp.concatenate([natural[pl.ds(s * PITCH, seg_len), :] for s in range(SEGS)], axis=0)


def entering(group, first, back_ref, rows_ref, local_ref, run, backward):
    big = rows_ref[0, group]
    state = rows_ref[1, group] * rows_of(back_ref, first + group, MODES, BACK)
    for s in reversed(range(SEGS)) if backward else range(SEGS):
        run[pl.ds(s, MODES, stride=SEGS), :] = local_ref[group, s] + state
        if s != (0 if backward else SEGS - 1):
            state = state * big


def far(total, indices, local_ref, group, k, step, chunks, lam_ref, mu_ref, run):
    for m in range(MODES):
        here = pl.ds(m * SEGS, SEGS)
        decay = lam_ref[group, m]
        state = run[here, :]
        c = state if step == 0 else local_ref[group, k, m] + state
        if step < chunks - 1:
            run[here, :] = state * mu_ref[group, m]
        for i in indices:
            total[i] = total[i] + c
            if i != indices[-1]:
                c = c * decay


def adjoint_block(
    group, seg_len, sq_ref, lam_ref, mu_ref, near_ref, rows_ref, al_ref, as_ref, back_ref,
    natural, run,
):
    chunks = seg_len // SUB
    entering(group, 8, back_ref, rows_ref, as_ref, run, True)
    for step in range(chunks):
        k = chunks - 1 - step
        near = [near_ref[group, d] for d in range(SUB)]
        ss = [sq_ref[group, k * SUB + j] for j in range(SUB)]
        total = []
        for j in range(SUB):
            value = near[0] * ss[j]
            for d in range(1, SUB - j):
                value = value + near[d] * ss[j + d]
            total.append(value)
        order = list(reversed(range(SUB)))
        far(total, order, al_ref, group, k, step, chunks, lam_ref, mu_ref, run)
        for j in range(SUB):
            natural[pl.ds(k * SUB + j, SEGS, stride=PITCH), :] = total[j]
    return natural_order(natural, seg_len).astype(jnp.bfloat16)


def back_kernel(
    sq_ref, lam_ref, mu_ref, near_ref, rows_ref, al_ref, as_ref, back_ref,
    ig_ref,
    natural, run,
):
    first, tokens, _ = ig_ref.shape

    def group_step(group, carry):
        ig_ref[group] = adjoint_block(
            group, tokens // SEGS, sq_ref, lam_ref, mu_ref, near_ref, rows_ref, al_ref, as_ref,
            back_ref, natural, run,
        )
        return carry

    lax.fori_loop(0, first, group_step, 0)


def gate_kernel(
    ig_buf, g_buf, xq_ref, sq_ref, lam_ref, mu_ref, near_ref, rows_ref,
    hl_ref, hs_ref, al_ref, as_ref, back_ref,
    ig_hbm, gg_hbm, late_ref,
    natural, run, ig_late, buf, ig_sem, sem,
):
    groups, tokens, _ = g_buf.shape
    first = ig_buf.shape[0]
    early = groups - LATE
    seg_len = tokens // SEGS
    chunks = seg_len // SUB

    def late_copy(group):
        return pltpu.make_async_copy(
            ig_late.at[group - first], ig_hbm.at[:, columns(group)], ig_sem.at[group]
        )

    for group in range(first):
        put(ig_hbm, ig_buf, ig_sem, group).start()

    def adjoint_step(group, carry):
        ig_late[group - first] = adjoint_block(
            group, seg_len, sq_ref, lam_ref, mu_ref, near_ref, rows_ref, al_ref, as_ref,
            back_ref, natural, run,
        )
        late_copy(group).start()
        return carry

    lax.fori_loop(first, groups, adjoint_step, 0)

    def group_step(group, carry):
        entering(group, 0, back_ref, rows_ref, hs_ref, run, False)
        for k in range(chunks):
            near = [near_ref[group, d] for d in range(SUB)]
            xs = [xq_ref[group, k * SUB + j] for j in range(SUB)]
            total = []
            for i in range(SUB):
                value = near[0] * xs[i]
                for d in range(1, i + 1):
                    value = value + near[d] * xs[i - d]
                total.append(value)
            far(total, list(range(SUB)), hl_ref, group, k, k, chunks, lam_ref, mu_ref, run)
            for i in range(SUB):
                natural[pl.ds(k * SUB + i, SEGS, stride=PITCH), :] = total[i]
        mixed = natural_order(natural, seg_len)
        gated = (g_buf[group].astype(F32) * mixed).astype(jnp.bfloat16)

        @pl.when(group < early)
        def _():
            buf[group] = gated
            put(gg_hbm, buf, sem, group).start()

        @pl.when(group >= early)
        def _():
            late_ref[group - early] = gated

        return carry

    lax.fori_loop(0, groups, group_step, 0)
    for group in range(groups):
        if group < first:
            put(ig_hbm, ig_buf, ig_sem, group).wait()
        else:
            late_copy(group).wait()
        if group < early:
            put(gg_hbm, buf, sem, group).wait()


def totals(back_ref, rows_ref, group):
    res_raw = rows_of(back_ref, 16 + group, MODES, BACK)
    log_raw = rows_ref[2, group] * rows_of(back_ref, 24 + group, MODES, BACK)
    return res_raw, log_raw


def skip_total(back_ref):
    total = back_ref[pl.ds(32, 8), :]
    for span in range(1, back_ref.shape[0] // BACK):
        total = total + back_ref[pl.ds(span * BACK + 32, 8), :]
    return total


def norm_kernel(back_ref, rows_ref, sq_ref):
    groups = rows_ref.shape[1]
    res_sq = jnp.zeros((MODES, LANES), F32)
    log_sq = jnp.zeros((MODES, LANES), F32)
    for group in range(groups):
        res_raw, log_raw = totals(back_ref, rows_ref, group)
        res_sq = res_sq + res_raw * res_raw
        log_sq = log_sq + log_raw * log_raw
    skip = skip_total(back_ref)
    rows = [jnp.sum(v, axis=0, keepdims=True) for v in (res_sq, log_sq, skip * skip)]
    sq_ref[...] = jnp.concatenate(rows + [jnp.zeros((5, LANES), F32)], axis=0)


def scale_kernel(
    own_ref, first_ref, second_ref, third_ref, back_ref, rows_ref, late_ref, part_hbm,
    rg_hbm, lg_hbm, sg_hbm, gg_hbm,
    rg_buf, lg_buf, sg_buf, late_sem, sem,
):
    groups = rows_ref.shape[1]
    copies = [
        pltpu.make_async_copy(
            late_ref.at[n], gg_hbm.at[:, columns(groups - LATE + n)], late_sem.at[n]
        )
        for n in range(LATE)
    ]
    for copy in copies:
        copy.start()
    total = (own_ref[...] + first_ref[...]) + (second_ref[...] + third_ref[...])
    sums = jnp.sum(total, axis=1, keepdims=True)

    def factor(n, ceiling):
        return jnp.minimum(1.0, ceiling / jnp.sqrt(sums[n : n + 1, :] + 1e-06))

    limit_modes = math.sqrt(MODES * CHANNELS)
    res_factor = factor(0, limit_modes)
    log_factor = factor(1, limit_modes)
    for group in range(groups):
        cols = pl.ds(group * LANES, LANES)
        res_raw, log_raw = totals(back_ref, rows_ref, group)
        rg_buf[:, cols] = res_raw * res_factor
        lg_buf[:, cols] = log_raw * log_factor
    sg_buf[...] = skip_total(back_ref) * factor(2, math.sqrt(CHANNELS))
    for n, (buf, hbm) in enumerate(((rg_buf, rg_hbm), (lg_buf, lg_hbm), (sg_buf, sg_hbm))):
        copy = pltpu.make_async_copy(buf, hbm, sem.at[n])
        copy.start()
        copies.append(copy)
    for copy in copies:
        copy.wait()


def params():
    return pltpu.CompilerParams(vmem_limit_bytes=VMEM_LIMIT)


def work(ops, moved):
    return pl.CostEstimate(flops=ops, bytes_accessed=moved, transcendentals=0)


HBM = pl.BlockSpec(memory_space=pltpu.HBM)
VMEM = pl.BlockSpec(memory_space=pltpu.VMEM)


def in_hbm(*arrays):
    return [pltpu.with_memory_space_constraint(array, pltpu.HBM) for array in arrays]


def shape(*dims):
    return jax.ShapeDtypeStruct(dims, F32)


def span_call(conv_input, out_gate, grad_out, pole_rate, residue, skip_gain):
    tokens, chan = conv_input.shape
    groups = chan // LANES
    seg_len = tokens // SEGS
    chunks = seg_len // SUB
    wide = pltpu.VMEM((AHEAD + 1, tokens, LANES), jnp.bfloat16)
    natural = pltpu.VMEM((SEGS * PITCH, LANES), F32)
    sems = pltpu.SemaphoreType.DMA((AHEAD + 1,))
    return pl.pallas_call(
        span_kernel,
        in_specs=[HBM] * 6,
        out_specs=[VMEM] * 13,
        out_shape=[
            shape(groups, chunks, MODES, SEGS, LANES),
            shape(groups, chunks, MODES, SEGS, LANES),
            shape(groups, SEGS, MODES, LANES),
            shape(groups, SEGS, MODES, LANES),
            shape(groups, seg_len, SEGS, LANES),
            shape(groups, seg_len, SEGS, LANES),
            shape(groups, MODES, SEGS, LANES),
            shape(groups, MODES, SEGS, LANES),
            shape(groups, SUB, SEGS, LANES),
            shape(4, groups, MODES, LANES),
            shape(groups, LANES),
            shape(MODES * SENT, LANES),
            jax.ShapeDtypeStruct((groups, tokens, LANES), jnp.bfloat16),
        ],
        scratch_shapes=[
            wide, wide,
            pltpu.VMEM((MODES, chan), F32),
            pltpu.VMEM((MODES, chan), F32),
            pltpu.VMEM((1, chan), F32),
            natural, natural,
            pltpu.VMEM((MODES, SEGS, LANES), F32),
            pltpu.VMEM((6, MODES * END_PITCH, LANES), F32),
            sems, sems, sems, pltpu.SemaphoreType.DMA((3,)),
        ],
        compiler_params=params(),
        name="span",
    )(
        *in_hbm(conv_input, out_gate, grad_out, pole_rate, residue, skip_gain.reshape(1, chan))
    )


def back_call(tokens, sq, lam, mu, near, rows, al, as_, back):
    groups = sq.shape[0]
    return pl.pallas_call(
        back_kernel,
        in_specs=[VMEM] * 8,
        out_specs=VMEM,
        out_shape=jax.ShapeDtypeStruct((min(FIRST, groups), tokens, LANES), jnp.bfloat16),
        scratch_shapes=[
            pltpu.VMEM((SEGS * PITCH, LANES), F32),
            pltpu.VMEM((MODES * SEGS, LANES), F32),
        ],
        compiler_params=params(),
        cost_estimate=work(40 * MODES * tokens * groups * LANES, 16 * tokens * groups * LANES),
        name="adjoint",
    )(sq, lam, mu, near, rows, al, as_, back)


def gate_call(ig, g, xq, sq, lam, mu, near, rows, hl, hs, al, as_, back):
    groups, tokens, _ = g.shape
    chan = groups * LANES
    sems = pltpu.SemaphoreType.DMA((groups,))
    return pl.pallas_call(
        gate_kernel,
        in_specs=[VMEM] * 13,
        out_specs=[HBM, HBM, VMEM],
        out_shape=[
            jax.ShapeDtypeStruct((tokens, chan), jnp.bfloat16),
            jax.ShapeDtypeStruct((tokens, chan), jnp.bfloat16),
            jax.ShapeDtypeStruct((LATE, tokens, LANES), jnp.bfloat16),
        ],
        scratch_shapes=[
            pltpu.VMEM((SEGS * PITCH, LANES), F32),
            pltpu.VMEM((MODES * SEGS, LANES), F32),
            pltpu.VMEM((groups - ig.shape[0], tokens, LANES), jnp.bfloat16),
            pltpu.VMEM((groups - LATE, tokens, LANES), jnp.bfloat16),
            sems, sems,
        ],
        compiler_params=params(),
        cost_estimate=work(40 * MODES * tokens * chan, 16 * tokens * chan),
        name="gate",
    )(ig, g, xq, sq, lam, mu, near, rows, hl, hs, al, as_, back)


def swapped(value, bit):
    peers = lax.axis_size("ch")
    return lax.ppermute(value, "ch", [(i, i ^ bit) for i in range(peers)])


def on_device(conv_input, out_gate, grad_out, pole_rate, residue, skip_gain):
    tokens, chan = conv_input.shape
    groups = chan // LANES
    spans = lax.axis_size("ctx")
    hl, al, hs, as_, xq, sq, lam, mu, near, rows, skip, pay, g = span_call(
        conv_input, out_gate, grad_out, pole_rate, residue, skip_gain
    )
    got = lax.all_to_all(pay.reshape(spans, SENT, LANES), "ctx", 0, 0)
    back = pl.pallas_call(
        functools.partial(chain_kernel, tokens),
        out_shape=shape(spans, BACK, LANES),
        compiler_params=params(),
        name="chain",
    )(got, rows, skip)
    back = lax.all_to_all(back, "ctx", 0, 0).reshape(MODES * BACK, LANES)

    squares = pl.pallas_call(
        norm_kernel,
        out_shape=shape(8, LANES),
        compiler_params=params(),
        name="norm",
    )(back, rows)
    squares = squares + swapped(squares, 1)
    others = [swapped(squares, bit) for bit in (6, 4, 2)]
    ig = back_call(tokens, sq, lam, mu, near, rows, al, as_, back)
    input_grad, gate_grad, late = gate_call(
        ig, g, xq, sq, lam, mu, near, rows, hl, hs, al, as_, back
    )
    *others, late = lax.optimization_barrier((*others, late))
    res_out, log_out, skip_out, gate_grad = pl.pallas_call(
        scale_kernel,
        in_specs=[VMEM] * 7 + [HBM],
        out_specs=[HBM] * 4,
        out_shape=[
            shape(MODES, chan), shape(MODES, chan), shape(groups, LANES),
            jax.ShapeDtypeStruct((tokens, chan), jnp.bfloat16),
        ],
        scratch_shapes=[
            pltpu.VMEM((MODES, chan), F32),
            pltpu.VMEM((MODES, chan), F32),
            pltpu.VMEM((groups, LANES), F32),
            pltpu.SemaphoreType.DMA((LATE,)),
            pltpu.SemaphoreType.DMA((3,)),
        ],
        input_output_aliases={7: 3},
        compiler_params=params(),
        name="scale",
    )(squares, *others, back, rows, late, gate_grad)
    return input_grad, gate_grad, res_out, log_out, skip_out.reshape(chan)


def solution(mesh):
    in_specs = (
        P("ctx", "ch"), P("ctx", "ch"), P("ctx", "ch"), P(None, "ch"), P(None, "ch"), P("ch"),
    )
    out_specs = (P("ctx", "ch"), P("ctx", "ch"), P(None, "ch"), P(None, "ch"), P("ch"))
    return jax.shard_map(
        on_device, mesh=mesh, in_specs=in_specs, out_specs=out_specs, check_vma=False
    )
```

```python
import functools
import math

import jax
import jax.numpy as jnp
from jax import lax
from jax.experimental import pallas as pl
from jax.experimental.pallas import tpu as pltpu
from jax.sharding import PartitionSpec as P

CHANNELS = 8192
MODES = 16
LANES = 128
SEGS = 8
SUB = 8
F32 = jnp.float32
FIRST = 6
LATE = 3
AHEAD = 2
END_PITCH = 9
SENT = 48
BACK = 40
PITCH = 72
VMEM_LIMIT = 16 * 1024 * 1024


def rows_of(ref, start, count, stride):
    return ref[pl.ds(start, count, stride=stride), :]


def spread(values):
    return jnp.broadcast_to(values, (SEGS, LANES))


def columns(group):
    return pl.ds(pl.multiple_of(group * LANES, LANES), LANES)


def span_kernel(
    x_hbm, o_hbm, g_hbm, rate_hbm, res_hbm, gain_hbm,
    hl_ref, al_ref, hs_ref, as_ref, xq_ref, sq_ref, lam_ref, mu_ref, near_ref, rows_ref, skip_ref, pay_ref, g_buf,
    x_buf, o_buf, rate_buf, res_buf, gain_buf,
    natural, second, rl_t, ends,
    x_sem, o_sem, g_sem, small_sem,
):
    tokens = x_buf.shape[1]
    groups = xq_ref.shape[0]
    seg_len = tokens // SEGS
    chunks = seg_len // SUB
    small = [
        pltpu.make_async_copy(hbm, buf, small_sem.at[n])
        for n, (hbm, buf) in enumerate(
            ((rate_hbm, rate_buf), (res_hbm, res_buf), (gain_hbm, gain_buf))
        )
    ]

    def blocks(group, slot):
        return [
            pltpu.make_async_copy(hbm.at[:, columns(group)], buf, sem.at[slot])
            for hbm, buf, sem in (
                (x_hbm, x_buf.at[slot], x_sem),
                (o_hbm, o_buf.at[slot], o_sem),
                (g_hbm, g_buf.at[group], g_sem),
            )
        ]

    for copy in blocks(0, 0) + small:
        copy.start()
    for group in range(1, min(AHEAD, groups)):
        for copy in blocks(group, group):
            copy.start()
    for copy in small:
        copy.wait()
    zero = jnp.zeros((SEGS, LANES), F32)

    def group_step(group, carry):
        slot = lax.rem(group, AHEAD + 1)

        @pl.when(group + AHEAD < groups)
        def _():
            for copy in blocks(group + AHEAD, lax.rem(group + AHEAD, AHEAD + 1)):
                copy.start()

        cols = columns(group)
        rate = rate_buf[:, cols]
        residue = res_buf[:, cols]
        lam = jnp.exp(-rate)
        mu_rows = jnp.exp(rate * (-float(SUB)))
        big = jnp.exp(rate * (-float(seg_len)))
        rl_rows = residue * lam
        for m in range(MODES):
            lam_ref[group, m] = spread(lam[m : m + 1, :])
            mu_ref[group, m] = spread(mu_rows[m : m + 1, :])
            rl_t[m] = spread(rl_rows[m : m + 1, :])
        rows_ref[0, group] = big
        rows_ref[1, group] = rl_rows
        rows_ref[2, group] = -(rate * residue)
        rows_ref[3, group] = rate
        term = residue
        for d in range(SUB):
            row = jnp.sum(term, axis=0, keepdims=True)
            if d == 0:
                row = row + gain_buf[:, cols]
            near_ref[group, d] = spread(row)
            term = term * lam

        xq = xq_ref.at[group]
        sq = sq_ref.at[group]
        for copy in blocks(group, slot):
            copy.wait()
        for s in range(SEGS):
            part = pl.ds(s * seg_len, seg_len)
            source = x_buf[slot, part, :].astype(F32)
            signal = g_buf[group, part, :].astype(F32) * o_buf[slot, part, :].astype(F32)
            natural[pl.ds(s * PITCH, seg_len), :] = source
            second[pl.ds(s * PITCH, seg_len), :] = signal

        def lag_step(k, acc):
            xs = [rows_of(natural, k * SUB + j, SEGS, PITCH) for j in range(SUB)]
            ss = [rows_of(second, k * SUB + j, SEGS, PITCH) for j in range(SUB)]
            for j in range(SUB):
                xq[k * SUB + j] = xs[j]
                sq[k * SUB + j] = ss[j]
            out = []
            for d in range(SUB):
                total = acc[d]
                for i in range(d, SUB):
                    total = total + ss[i] * xs[i - d]
                out.append(total)
            return tuple(out)

        lagged = lax.fori_loop(0, chunks, lag_step, (zero,) * SUB, unroll=8)
        lag_rows = [jnp.sum(v, axis=0, keepdims=True) for v in lagged]
        skip_ref[pl.ds(group, 1), :] = lag_rows[0]
        res_near = jnp.broadcast_to(lag_rows[0], lam.shape)
        log_near = jnp.zeros_like(lam)
        power = lam
        for d in range(1, SUB):
            term = power * lag_rows[d]
            res_near = res_near + term
            log_near = log_near + float(d) * term
            power = power * lam

        def mode_step(m, carry):
            p1 = lam_ref[group, m]
            mu = mu_ref[group, m]
            rl = rl_t[m]
            p2 = p1 * p1
            p3 = p2 * p1
            p4 = p2 * p2
            pw = [None, p1, p2, p3, p4, p4 * p1, p3 * p3, p4 * p3]
            a_parts = [None] * chunks
            b_parts = [None] * chunks
            for k in reversed(range(chunks)):
                a = sq[k * SUB + SUB - 1] * pw[SUB - 1]
                b = a
                for i in reversed(range(1, SUB - 1)):
                    a = a + sq[k * SUB + i] * pw[i]
                    b = b + a
                a = a + sq[k * SUB]
                a_parts[k] = a
                b_parts[k] = b
                if k == chunks - 1:
                    al_ref[group, k, m] = zero
                    a_run = a
                    b_run = b
                else:
                    al_ref[group, k, m] = rl * a_run
                    b_run = b + mu * (b_run + float(SUB) * a_run)
                    a_run = a + mu * a_run
            for k in range(chunks):
                h = xq[k * SUB] * pw[SUB - 1]
                p = h
                for j in range(1, SUB - 1):
                    h = h + xq[k * SUB + j] * pw[SUB - 1 - j]
                    p = p + h
                h = h + xq[k * SUB + SUB - 1]
                if k == 0:
                    hl_ref[group, k, m] = zero
                    h_run = h
                    p_run = p
                    continue
                hl_ref[group, k, m] = rl * h_run
                res_new = h_run * a_parts[k]
                log_new = p_run * a_parts[k] + h_run * b_parts[k]
                res_x = res_new if k == 1 else res_x + res_new
                log_x = log_new if k == 1 else log_x + log_new
                p_run = p + mu * (p_run + float(SUB) * h_run)
                h_run = h + mu * h_run
            for n, value in enumerate((h_run, p_run, a_run, b_run, res_x, log_x)):
                ends[n, pl.ds(m * END_PITCH, SEGS), :] = value
            return carry

        lax.fori_loop(0, MODES, mode_step, 0, unroll=16)

        def end(n, s):
            return ends[n, pl.ds(s, MODES, stride=END_PITCH), :]

        span = float(seg_len)
        nothing = jnp.zeros_like(lam)
        h, p, res_x, log_x = nothing, nothing, nothing, nothing
        for s in range(SEGS):
            hs_ref[group, s] = rl_rows * h
            a_s, b_s = end(2, s), end(3, s)
            res_x = res_x + end(4, s) + h * a_s
            log_x = log_x + end(5, s) + (p * a_s + h * b_s)
            p = end(1, s) + big * (p + span * h)
            h = end(0, s) + big * h
        a, b = nothing, nothing
        for s in reversed(range(SEGS)):
            as_ref[group, s] = rl_rows * a
            b = end(3, s) + big * (b + span * a)
            a = end(2, s) + big * a
        res_sum = lam * res_x + res_near
        log_sum = lam * (log_x + res_x) + log_near
        rows = (h, p, a, b, res_sum, log_sum)
        for n, value in enumerate(rows):
            pay_ref[pl.ds(n * 8 + group, MODES, stride=SENT), :] = value
        return carry

    lax.fori_loop(0, groups, group_step, 0)


def chain_kernel(tokens, got_ref, rows_ref, skip_ref, back_ref):
    spans = got_ref.shape[0]
    groups = skip_ref.shape[0]
    own = lax.axis_index("ctx")

    def part(d, n):
        return got_ref[d, pl.ds(8 * n, 8), :]

    rate = jnp.concatenate(
        [rows_ref[3, group, pl.ds(own, 1), :] for group in range(groups)], axis=0
    )
    lam = jnp.exp(-rate)
    big = jnp.exp(rate * (-float(tokens)))
    span = float(tokens)
    zero = jnp.zeros((8, LANES), F32)
    h, p, res_x, log_x, res_sum, log_sum = (zero,) * 6
    for d in range(spans):
        back_ref[d, pl.ds(0, 8), :] = h
        a_d = part(d, 2)
        res_x = res_x + h * a_d
        log_x = log_x + (p * a_d + h * part(d, 3))
        res_sum = res_sum + part(d, 4)
        log_sum = log_sum + part(d, 5)
        p = part(d, 1) + big * (p + span * h)
        h = part(d, 0) + big * h
    a = zero
    for d in reversed(range(spans)):
        back_ref[d, pl.ds(8, 8), :] = a
        a = part(d, 2) + big * a
    res_total = res_sum + lam * res_x
    log_total = log_sum + lam * (log_x + res_x)
    for d in range(spans):
        back_ref[d, pl.ds(16, 8), :] = res_total
        back_ref[d, pl.ds(24, 8), :] = log_total
        back_ref[d, pl.ds(32, 8), :] = skip_ref[...]


def put(hbm, buf, sem, group):
    return pltpu.make_async_copy(buf.at[group], hbm.at[:, columns(group)], sem.at[group])


def natural_order(natural, seg_len):
    return jnp.concatenate([natural[pl.ds(s * PITCH, seg_len), :] for s in range(SEGS)], axis=0)


def entering(group, first, back_ref, rows_ref, local_ref, run, backward):
    big = rows_ref[0, group]
    state = rows_ref[1, group] * rows_of(back_ref, first + group, MODES, BACK)
    for s in reversed(range(SEGS)) if backward else range(SEGS):
        run[pl.ds(s, MODES, stride=SEGS), :] = local_ref[group, s] + state
        if s != (0 if backward else SEGS - 1):
            state = state * big


def far(total, indices, local_ref, group, k, step, chunks, lam_ref, mu_ref, run):
    for m in range(MODES):
        here = pl.ds(m * SEGS, SEGS)
        decay = lam_ref[group, m]
        state = run[here, :]
        c = state if step == 0 else local_ref[group, k, m] + state
        if step < chunks - 1:
            run[here, :] = state * mu_ref[group, m]
        for i in indices:
            total[i] = total[i] + c
            if i != indices[-1]:
                c = c * decay


def adjoint_block(
    group, seg_len, sq_ref, lam_ref, mu_ref, near_ref, rows_ref, al_ref, as_ref, back_ref,
    natural, run,
):
    chunks = seg_len // SUB
    entering(group, 8, back_ref, rows_ref, as_ref, run, True)
    for step in range(chunks):
        k = chunks - 1 - step
        near = [near_ref[group, d] for d in range(SUB)]
        ss = [sq_ref[group, k * SUB + j] for j in range(SUB)]
        total = []
        for j in range(SUB):
            value = near[0] * ss[j]
            for d in range(1, SUB - j):
                value = value + near[d] * ss[j + d]
            total.append(value)
        order = list(reversed(range(SUB)))
        far(total, order, al_ref, group, k, step, chunks, lam_ref, mu_ref, run)
        for j in range(SUB):
            natural[pl.ds(k * SUB + j, SEGS, stride=PITCH), :] = total[j]
    return natural_order(natural, seg_len).astype(jnp.bfloat16)


def back_kernel(
    sq_ref, lam_ref, mu_ref, near_ref, rows_ref, al_ref, as_ref, back_ref,
    ig_ref,
    natural, run,
):
    first, tokens, _ = ig_ref.shape

    def group_step(group, carry):
        ig_ref[group] = adjoint_block(
            group, tokens // SEGS, sq_ref, lam_ref, mu_ref, near_ref, rows_ref, al_ref, as_ref,
            back_ref, natural, run,
        )
        return carry

    lax.fori_loop(0, first, group_step, 0)


def gate_kernel(
    ig_buf, g_buf, xq_ref, sq_ref, lam_ref, mu_ref, near_ref, rows_ref,
    hl_ref, hs_ref, al_ref, as_ref, back_ref,
    ig_hbm, gg_hbm, late_ref,
    natural, run, ig_late, buf, ig_sem, sem,
):
    groups, tokens, _ = g_buf.shape
    first = ig_buf.shape[0]
    early = groups - LATE
    seg_len = tokens // SEGS
    chunks = seg_len // SUB

    def late_copy(group):
        return pltpu.make_async_copy(
            ig_late.at[group - first], ig_hbm.at[:, columns(group)], ig_sem.at[group]
        )

    for group in range(first):
        put(ig_hbm, ig_buf, ig_sem, group).start()

    def adjoint_step(group, carry):
        ig_late[group - first] = adjoint_block(
            group, seg_len, sq_ref, lam_ref, mu_ref, near_ref, rows_ref, al_ref, as_ref,
            back_ref, natural, run,
        )
        late_copy(group).start()
        return carry

    lax.fori_loop(first, groups, adjoint_step, 0)

    def group_step(group, carry):
        entering(group, 0, back_ref, rows_ref, hs_ref, run, False)
        for k in range(chunks):
            near = [near_ref[group, d] for d in range(SUB)]
            xs = [xq_ref[group, k * SUB + j] for j in range(SUB)]
            total = []
            for i in range(SUB):
                value = near[0] * xs[i]
                for d in range(1, i + 1):
                    value = value + near[d] * xs[i - d]
                total.append(value)
            far(total, list(range(SUB)), hl_ref, group, k, k, chunks, lam_ref, mu_ref, run)
            for i in range(SUB):
                natural[pl.ds(k * SUB + i, SEGS, stride=PITCH), :] = total[i]
        mixed = natural_order(natural, seg_len)
        gated = (g_buf[group].astype(F32) * mixed).astype(jnp.bfloat16)

        @pl.when(group < early)
        def _():
            buf[group] = gated
            put(gg_hbm, buf, sem, group).start()

        @pl.when(group >= early)
        def _():
            late_ref[group - early] = gated

        return carry

    lax.fori_loop(0, groups, group_step, 0)
    for group in range(groups):
        if group < first:
            put(ig_hbm, ig_buf, ig_sem, group).wait()
        else:
            late_copy(group).wait()
        if group < early:
            put(gg_hbm, buf, sem, group).wait()


def totals(back_ref, rows_ref, group):
    res_raw = rows_of(back_ref, 16 + group, MODES, BACK)
    log_raw = rows_ref[2, group] * rows_of(back_ref, 24 + group, MODES, BACK)
    return res_raw, log_raw


def skip_total(back_ref):
    total = back_ref[pl.ds(32, 8), :]
    for span in range(1, back_ref.shape[0] // BACK):
        total = total + back_ref[pl.ds(span * BACK + 32, 8), :]
    return total


def norm_kernel(back_ref, rows_ref, sq_ref):
    groups = rows_ref.shape[1]
    res_sq = jnp.zeros((MODES, LANES), F32)
    log_sq = jnp.zeros((MODES, LANES), F32)
    for group in range(groups):
        res_raw, log_raw = totals(back_ref, rows_ref, group)
        res_sq = res_sq + res_raw * res_raw
        log_sq = log_sq + log_raw * log_raw
    skip = skip_total(back_ref)
    rows = [jnp.sum(v, axis=0, keepdims=True) for v in (res_sq, log_sq, skip * skip)]
    sq_ref[...] = jnp.concatenate(rows + [jnp.zeros((5, LANES), F32)], axis=0)


def scale_kernel(
    own_ref, first_ref, second_ref, third_ref, back_ref, rows_ref, late_ref, part_hbm,
    rg_hbm, lg_hbm, sg_hbm, gg_hbm,
    rg_buf, lg_buf, sg_buf, late_sem, sem,
):
    groups = rows_ref.shape[1]
    copies = [
        pltpu.make_async_copy(
            late_ref.at[n], gg_hbm.at[:, columns(groups - LATE + n)], late_sem.at[n]
        )
        for n in range(LATE)
    ]
    for copy in copies:
        copy.start()
    total = (own_ref[...] + first_ref[...]) + (second_ref[...] + third_ref[...])
    sums = jnp.sum(total, axis=1, keepdims=True)

    def factor(n, ceiling):
        return jnp.minimum(1.0, ceiling / jnp.sqrt(sums[n : n + 1, :] + 1e-06))

    limit_modes = math.sqrt(MODES * CHANNELS)
    res_factor = factor(0, limit_modes)
    log_factor = factor(1, limit_modes)
    for group in range(groups):
        cols = pl.ds(group * LANES, LANES)
        res_raw, log_raw = totals(back_ref, rows_ref, group)
        rg_buf[:, cols] = res_raw * res_factor
        lg_buf[:, cols] = log_raw * log_factor
    sg_buf[...] = skip_total(back_ref) * factor(2, math.sqrt(CHANNELS))
    for n, (buf, hbm) in enumerate(((rg_buf, rg_hbm), (lg_buf, lg_hbm), (sg_buf, sg_hbm))):
        copy = pltpu.make_async_copy(buf, hbm, sem.at[n])
        copy.start()
        copies.append(copy)
    for copy in copies:
        copy.wait()


def params():
    return pltpu.CompilerParams(vmem_limit_bytes=VMEM_LIMIT)


def work(ops, moved):
    return pl.CostEstimate(flops=ops, bytes_accessed=moved, transcendentals=0)


HBM = pl.BlockSpec(memory_space=pltpu.HBM)
VMEM = pl.BlockSpec(memory_space=pltpu.VMEM)


def in_hbm(*arrays):
    return [pltpu.with_memory_space_constraint(array, pltpu.HBM) for array in arrays]


def shape(*dims):
    return jax.ShapeDtypeStruct(dims, F32)


def span_call(conv_input, out_gate, grad_out, pole_rate, residue, skip_gain):
    tokens, chan = conv_input.shape
    groups = chan // LANES
    seg_len = tokens // SEGS
    chunks = seg_len // SUB
    wide = pltpu.VMEM((AHEAD + 1, tokens, LANES), jnp.bfloat16)
    natural = pltpu.VMEM((SEGS * PITCH, LANES), F32)
    sems = pltpu.SemaphoreType.DMA((AHEAD + 1,))
    return pl.pallas_call(
        span_kernel,
        in_specs=[HBM] * 6,
        out_specs=[VMEM] * 13,
        out_shape=[
            shape(groups, chunks, MODES, SEGS, LANES),
            shape(groups, chunks, MODES, SEGS, LANES),
            shape(groups, SEGS, MODES, LANES),
            shape(groups, SEGS, MODES, LANES),
            shape(groups, seg_len, SEGS, LANES),
            shape(groups, seg_len, SEGS, LANES),
            shape(groups, MODES, SEGS, LANES),
            shape(groups, MODES, SEGS, LANES),
            shape(groups, SUB, SEGS, LANES),
            shape(4, groups, MODES, LANES),
            shape(groups, LANES),
            shape(MODES * SENT, LANES),
            jax.ShapeDtypeStruct((groups, tokens, LANES), jnp.bfloat16),
        ],
        scratch_shapes=[
            wide, wide,
            pltpu.VMEM((MODES, chan), F32),
            pltpu.VMEM((MODES, chan), F32),
            pltpu.VMEM((1, chan), F32),
            natural, natural,
            pltpu.VMEM((MODES, SEGS, LANES), F32),
            pltpu.VMEM((6, MODES * END_PITCH, LANES), F32),
            sems, sems, sems, pltpu.SemaphoreType.DMA((3,)),
        ],
        compiler_params=params(),
        name="span",
    )(
        *in_hbm(conv_input, out_gate, grad_out, pole_rate, residue, skip_gain.reshape(1, chan))
    )


def back_call(tokens, sq, lam, mu, near, rows, al, as_, back):
    groups = sq.shape[0]
    return pl.pallas_call(
        back_kernel,
        in_specs=[VMEM] * 8,
        out_specs=VMEM,
        out_shape=jax.ShapeDtypeStruct((min(FIRST, groups), tokens, LANES), jnp.bfloat16),
        scratch_shapes=[
            pltpu.VMEM((SEGS * PITCH, LANES), F32),
            pltpu.VMEM((MODES * SEGS, LANES), F32),
        ],
        compiler_params=params(),
        cost_estimate=work(40 * MODES * tokens * groups * LANES, 16 * tokens * groups * LANES),
        name="adjoint",
    )(sq, lam, mu, near, rows, al, as_, back)


def gate_call(ig, g, xq, sq, lam, mu, near, rows, hl, hs, al, as_, back):
    groups, tokens, _ = g.shape
    chan = groups * LANES
    sems = pltpu.SemaphoreType.DMA((groups,))
    return pl.pallas_call(
        gate_kernel,
        in_specs=[VMEM] * 13,
        out_specs=[HBM, HBM, VMEM],
        out_shape=[
            jax.ShapeDtypeStruct((tokens, chan), jnp.bfloat16),
            jax.ShapeDtypeStruct((tokens, chan), jnp.bfloat16),
            jax.ShapeDtypeStruct((LATE, tokens, LANES), jnp.bfloat16),
        ],
        scratch_shapes=[
            pltpu.VMEM((SEGS * PITCH, LANES), F32),
            pltpu.VMEM((MODES * SEGS, LANES), F32),
            pltpu.VMEM((groups - ig.shape[0], tokens, LANES), jnp.bfloat16),
            pltpu.VMEM((groups - LATE, tokens, LANES), jnp.bfloat16),
            sems, sems,
        ],
        compiler_params=params(),
        cost_estimate=work(40 * MODES * tokens * chan, 16 * tokens * chan),
        name="gate",
    )(ig, g, xq, sq, lam, mu, near, rows, hl, hs, al, as_, back)


def swapped(value, bit):
    peers = lax.axis_size("ch")
    return lax.ppermute(value, "ch", [(i, i ^ bit) for i in range(peers)])


def on_device(conv_input, out_gate, grad_out, pole_rate, residue, skip_gain):
    tokens, chan = conv_input.shape
    groups = chan // LANES
    spans = lax.axis_size("ctx")
    hl, al, hs, as_, xq, sq, lam, mu, near, rows, skip, pay, g = span_call(
        conv_input, out_gate, grad_out, pole_rate, residue, skip_gain
    )
    got = lax.all_to_all(pay.reshape(spans, SENT, LANES), "ctx", 0, 0)
    back = pl.pallas_call(
        functools.partial(chain_kernel, tokens),
        out_shape=shape(spans, BACK, LANES),
        compiler_params=params(),
        name="chain",
    )(got, rows, skip)
    back = lax.all_to_all(back, "ctx", 0, 0).reshape(MODES * BACK, LANES)

    squares = pl.pallas_call(
        norm_kernel,
        out_shape=shape(8, LANES),
        compiler_params=params(),
        name="norm",
    )(back, rows)
    squares = squares + swapped(squares, 1)
    others = [swapped(squares, bit) for bit in (6, 4, 2)]
    ig = back_call(tokens, sq, lam, mu, near, rows, al, as_, back)
    input_grad, gate_grad, late = gate_call(
        ig, g, xq, sq, lam, mu, near, rows, hl, hs, al, as_, back
    )
    *others, late = lax.optimization_barrier((*others, late))
    res_out, log_out, skip_out, gate_grad = pl.pallas_call(
        scale_kernel,
        in_specs=[VMEM] * 7 + [HBM],
        out_specs=[HBM] * 4,
        out_shape=[
            shape(MODES, chan), shape(MODES, chan), shape(groups, LANES),
            jax.ShapeDtypeStruct((tokens, chan), jnp.bfloat16),
        ],
        scratch_shapes=[
            pltpu.VMEM((MODES, chan), F32),
            pltpu.VMEM((MODES, chan), F32),
            pltpu.VMEM((groups, LANES), F32),
            pltpu.SemaphoreType.DMA((LATE,)),
            pltpu.SemaphoreType.DMA((3,)),
        ],
        input_output_aliases={7: 3},
        compiler_params=params(),
        name="scale",
    )(squares, *others, back, rows, late, gate_grad)
    return input_grad, gate_grad, res_out, log_out, skip_out.reshape(chan)


def solution(mesh):
    in_specs = (
        P("ctx", "ch"), P("ctx", "ch"), P("ctx", "ch"), P(None, "ch"), P(None, "ch"), P("ch"),
    )
    out_specs = (P("ctx", "ch"), P("ctx", "ch"), P(None, "ch"), P(None, "ch"), P("ch"))
    return jax.shard_map(
        on_device, mesh=mesh, in_specs=in_specs, out_specs=out_specs, check_vma=False
    )
```
